256 devices in a mesh: island: 32 (over z, y_hi, core), tensor: 8 (over x, y_lo).
Axes of the slice: x: 4, y: 4 (y_hi: 2, y_lo: 2; y = y_hi * 2 + y_lo), z: 8, core: 2. Of those that a mesh axis runs over, the one named last changes fastest.
Arguments:
- hidden_rows: bfloat16 [32, 1024, 4096], P('island', 'tensor'), may hold values from -6 to 6
- queries: bfloat16 [32, 1024, 4096], P('island', None, 'tensor')
- key_states: bfloat16 [32, 1024, 1024], P('island', None, 'tensor')
- out_grads: bfloat16 [32, 1024, 4096], P('island', None, 'tensor'), may hold values from -6 to 6
- doc_ids: int32 [32, 1024], P('island'), may hold values from 0 to 3, never falling along the last dimension, each value on 1 to 512 neighbouring positions
- value_weight: bfloat16 [4096, 1024], P(None, 'tensor'), may hold values from -0.09375 to 0.09375
- momentum: float32 [4096, 1024], P(None, 'tensor'), may hold values from -0.015625 to 0.015625
- keep_index: int32 [4096, 8, 8], P(None, 'tensor'), may hold values from 0 to 127, all different within a row
Outputs:
- new_weight: bfloat16 [4096, 1024], P(None, 'tensor')
- new_momentum: float32 [4096, 1024], P(None, 'tensor')
The draws below stay inside these ranges and needn't reach their ends.
Inputs may be any that keep to these rules, and one draw needn't show every extreme that they name: `keep_index`: the 8 indices of one span are distinct. `doc_ids`: ids never fall along a sequence.
All inputs are finite; a program needn't handle non-finite values.
Results may differ from the reference program's by a relative error of at most 0.0041.
Values may be sent and summed in bfloat16 or wider, within the bound.
No kernel may reach another device: no remote copies, remote signals or barrier semaphores. Data moves between devices by JAX's collectives and lax.ppermute only.
A program may use at most 128 MiB of HBM per device.

```python
import math
import jax
import jax.numpy as jnp
import numpy as np
from jax import lax

D = 4096
Q_HEADS = 32
KV_HEADS = 8
HEAD_DIM = 128
SEQ = 1024
KEEP = 8
DOCS = 4
ISLANDS = 32


def shared_keys(key):
    return jax.random.normal(key, (ISLANDS, SEQ, KV_HEADS * HEAD_DIM), jnp.float32)


def draw_key_states(key, part):
    base = shared_keys(key)
    return base.astype(jnp.bfloat16)


def draw_queries(key, part):
    key = jax.random.fold_in(key, 9)
    drawn = jax.random.normal(key, (ISLANDS, SEQ, Q_HEADS * HEAD_DIM), jnp.float32)
    return drawn.astype(jnp.bfloat16)


def block_levels(own_key, shape, cuts, least, high):
    factor_of, own = 1.0, jax.random.fold_in(own_key, 6)
    for dim, blocks in cuts:
        steps = jnp.exp(jax.random.uniform(jax.random.fold_in(own, dim), (blocks,), jnp.float32, least / len(cuts), high / len(cuts)))
        factor_of = factor_of * jnp.repeat(steps, shape[dim] // blocks).reshape([-1 if axis == dim else 1 for axis in range(len(shape))])
    return factor_of


def distinct(own_key, rows, number_of, top, lift):
    sequence = jax.random.permutation(jax.random.fold_in(own_key, 1), number_of)
    boost = sequence
    for power in range(3):
        boost = boost * boost // number_of
    boost = boost * lift // number_of
    tickets = jax.random.randint(jax.random.fold_in(own_key, 2), (rows, number_of), 0, 4096) + boost
    holders = jax.random.permutation(jax.random.fold_in(own_key, 3), rows)[jnp.arange(number_of) % rows]
    tickets = jnp.where(jnp.arange(rows)[:, None] == holders[None, :], 1 << 14, tickets)
    merit = tickets * number_of + jnp.arange(number_of)
    return lax.top_k(merit.astype(jnp.int32), top)[1].astype(jnp.int32)


def length_profile(number_of, total, bound, slope):
    portions = [(1 << 20) // math.isqrt(standing ** slope) + 1 for standing in range(2, number_of + 1)]
    rest, given = total - bound - (number_of - 1), [1] * (number_of - 1)
    while rest > 0:
        free = [i for i in range(number_of - 1) if given[i] < bound]
        whole, left = sum([portions[i] for i in free]), rest
        for i in free:
            addition = min(bound - given[i], max(1, left * portions[i] // whole), rest)
            given[i] = given[i] + addition
            rest = rest - addition
    return np.array([bound] + given)


def uneven(rng, amount, total, limit, skew):
    if amount == 2:
        one = jax.random.randint(rng, (), max(1, total - limit), min(limit, total - 1) + 1)
        return jnp.stack([one, total - one])
    tallies = jnp.asarray(length_profile(amount, total, limit, skew), jnp.int32)
    twos = (amount - 1) // 2
    donor, receiver = tallies[1:1 + 2 * twos:2], tallies[2:2 + 2 * twos:2]
    room = jnp.minimum(donor - 1, limit - receiver)
    passed = jax.random.randint(jax.random.fold_in(rng, 1), (twos,), 0, 1 << 20) % (room + 1)
    tallies = tallies.at[1:1 + 2 * twos:2].set(donor - passed).at[2:2 + 2 * twos:2].set(receiver + passed)
    return tallies[jax.random.permutation(jax.random.fold_in(rng, 2), amount)]


def gaussian(own_key, extent, scale, bound, split=(), held_as=jnp.bfloat16):
    entries = scale * jax.random.normal(own_key, extent, jnp.float32)
    if split:
        entries = entries * block_levels(own_key, extent, split, -0.22, 0.18)
    return jnp.clip(entries, -bound, bound).astype(held_as)


def setup_inputs(seed: int = 0) -> dict:
    arg_keys = jax.random.split(jax.random.key(seed), 9)
    return {
        "hidden_rows": gaussian(arg_keys[0], (ISLANDS, SEQ, D), 1.0, 6.0, ((0, 32), (1, 8))),
        "queries": draw_queries(jax.random.fold_in(arg_keys[8], 71), 0),
        "key_states": draw_key_states(jax.random.fold_in(arg_keys[8], 71), 0),
        "out_grads": gaussian(arg_keys[3], (ISLANDS, SEQ, Q_HEADS * HEAD_DIM), 1.0, 6.0, ((0, 32), (2, 8))),
        "doc_ids": jax.vmap(lambda own: jnp.searchsorted(jnp.cumsum(uneven(own, DOCS, SEQ, SEQ // 2, 0)), jnp.arange(SEQ), side="right"))(jax.random.split(arg_keys[4], ISLANDS)).reshape((ISLANDS, SEQ)).astype(jnp.int32),
        "value_weight": gaussian(arg_keys[5], (D, KV_HEADS * HEAD_DIM), D ** -0.5, 0.09375, ((1, 8),)),
        "momentum": gaussian(arg_keys[6], (D, KV_HEADS * HEAD_DIM), 0.003, 0.015625, ((1, 8),), jnp.float32),
        "keep_index": distinct(arg_keys[7], D * KV_HEADS, HEAD_DIM, KEEP, 0).reshape((D, KV_HEADS, KEEP)),
    }


inner_rate = 0.01
outer_rate = 0.7
momentum_beta = 0.9
masked_score = -1e+30

def dct_table(length):
    frequency = jnp.arange(length, dtype=jnp.float32)[:, None]
    sample = jnp.arange(length, dtype=jnp.float32)[None, :]
    basis = jnp.cos(math.pi * (sample + 0.5) * frequency / length)
    return basis * jnp.where(frequency == 0.0, math.sqrt(1.0 / length), math.sqrt(2.0 / length))

def value_grads(queries, key_states, out_grads, doc_ids):
    length = key_states.shape[0]
    heads_kv = key_states.shape[1] // HEAD_DIM
    group = queries.shape[1] // key_states.shape[1]
    block = min(length, 512)
    count = length // block
    keys_split = key_states.reshape(length, heads_kv, HEAD_DIM).astype(jnp.float32)
    query_blocks = queries.reshape(count, block, heads_kv, group, HEAD_DIM)
    grad_blocks = out_grads.reshape(count, block, heads_kv, group, HEAD_DIM)
    doc_blocks = doc_ids.reshape(count, block)
    offsets = jnp.arange(count, dtype=jnp.int32) * block
    columns = jnp.arange(length, dtype=jnp.int32)
    scale = HEAD_DIM ** (-0.5)

    def step(totals, inputs):
        query_block, grad_block, doc_block, offset = inputs
        scores = jnp.einsum('bhgd,shd->hgbs', query_block.astype(jnp.float32), keys_split) * scale
        rows_here = offset + jnp.arange(block, dtype=jnp.int32)
        allowed = (doc_block[:, None] == doc_ids[None, :]) & (columns[None, :] <= rows_here[:, None])
        scores = jnp.where(allowed[None, None], scores, masked_score)
        peak = lax.optimization_barrier(jnp.max(scores, axis=3, keepdims=True))
        weights = jnp.exp(scores - peak)
        probs = (weights / lax.optimization_barrier(jnp.sum(weights, axis=3, keepdims=True))).astype(jnp.bfloat16)
        totals = totals + jnp.einsum('hgbs,bhgd->shd', probs.astype(jnp.float32), grad_block.astype(jnp.float32))
        return (totals, None)
    start = jnp.zeros((length, heads_kv, HEAD_DIM), jnp.float32)
    totals, unused = lax.scan(step, start, (query_blocks, grad_blocks, doc_blocks, offsets))
    return totals.reshape(length, heads_kv * HEAD_DIM).astype(jnp.bfloat16)

def encode(pseudo, keep_index, table):
    length = table.shape[0]
    spans = pseudo.reshape(pseudo.shape[0], keep_index.shape[1], length)
    coeffs = jnp.einsum('rhn,kn->rhk', spans, table, precision=lax.Precision.HIGHEST)
    picker = keep_index[:, :, :, None] == jnp.arange(length, dtype=jnp.int32)[None, None, None, :]
    return lax.optimization_barrier(jnp.sum(jnp.where(picker, coeffs[:, :, None, :], 0.0), axis=3))

def decode(kept, keep_index, table):
    length = table.shape[0]
    picker = keep_index[:, :, :, None] == jnp.arange(length, dtype=jnp.int32)[None, None, None, :]
    dense = lax.optimization_barrier(jnp.sum(jnp.where(picker, kept[:, :, :, None], 0.0), axis=2))
    spans = jnp.einsum('rhk,kn->rhn', dense, table, precision=lax.Precision.HIGHEST)
    return spans.reshape(kept.shape[0], keep_index.shape[1] * length)

def reference(hidden_rows, queries, key_states, out_grads, doc_ids, value_weight, momentum, keep_index):
    table = dct_table(HEAD_DIM)

    def island_kept(inputs):
        layer_rows, query_rows, key_rows, grad_rows, documents = inputs
        values = value_grads(query_rows, key_rows, grad_rows, documents)
        weight_grad = jnp.dot(layer_rows.T, values, preferred_element_type=jnp.float32)
        return encode(inner_rate * weight_grad, keep_index, table)
    kept = lax.map(island_kept, (hidden_rows, queries, key_states, out_grads, doc_ids))
    mean_kept = lax.optimization_barrier(jnp.sum(kept, axis=0)) / ISLANDS
    delta = decode(mean_kept, keep_index, table)
    new_momentum = momentum_beta * momentum + delta
    new_weight = (value_weight.astype(jnp.float32) - outer_rate * (delta + momentum_beta * new_momentum)).astype(jnp.bfloat16)
    return (new_weight, new_momentum)
```

```python
import functools
import math

import jax
import jax.numpy as jnp
import numpy as np
from jax import lax
from jax.experimental import pallas as pl
from jax.experimental.pallas import tpu as pltpu
from jax.sharding import Mesh
from jax.sharding import PartitionSpec as P

HEAD_DIM = 128
KEEP = 8
SPAN = 512
ROWS = 256

inner_rate = 0.01
outer_rate = 0.7
momentum_beta = 0.9
masked_score = -1e30
exp2_scale = HEAD_DIM ** (-0.5) / math.log(2.0)

BF16 = jnp.bfloat16
F32 = jnp.float32
LAST = (((1,), (1,)), ((), ()))
PLAIN = (((1,), (0,)), ((), ()))
FIRST = (((0,), (0,)), ((), ()))
MIB = 1 << 20


def dot(a, b, dims):
    return lax.dot_general(a, b, dims, preferred_element_type=F32)


def dct_tables():
    frequency = np.arange(HEAD_DIM, dtype=np.float64)[:, None]
    sample = np.arange(HEAD_DIM, dtype=np.float64)[None, :]
    basis = np.cos(np.pi * (sample + 0.5) * frequency / HEAD_DIM)
    table = basis * np.where(frequency == 0.0, math.sqrt(1.0 / HEAD_DIM), math.sqrt(2.0 / HEAD_DIM))
    high = table.astype(jnp.bfloat16)
    low = (table - high.astype(np.float64)).astype(jnp.bfloat16)
    return high, low


def grads_kernel(doc_ref, q_ref, k_ref, g_ref, index_ref, out_ref, cap_ref, total_ref):
    length = k_ref.shape[0]
    group = q_ref.shape[1] // HEAD_DIM
    docs = doc_ref[...]
    first = jnp.zeros_like(docs)
    for ident in (1, 2, 3):
        before = jnp.sum((docs < ident).astype(jnp.int32), axis=1, keepdims=True)
        first = jnp.where(docs == ident, before, first)
    total_ref[...] = jnp.zeros_like(total_ref)
    for row in range(0, length, ROWS):
        low = max(0, row - SPAN)
        width = row + ROWS - low
        start = first[:, row : row + ROWS]
        key = lax.broadcasted_iota(jnp.int32, (width, ROWS), 0) + low
        query = lax.broadcasted_iota(jnp.int32, (width, ROWS), 1) + row
        allowed = (key >= start) & (key <= query)
        cap_ref[:width] = jnp.where(allowed, jnp.finfo(F32).max, masked_score)
        for head in range(group):
            lanes = slice(head * HEAD_DIM, (head + 1) * HEAD_DIM)
            scores = dot(k_ref[low : row + ROWS], q_ref[row : row + ROWS, lanes], LAST)
            scores = jnp.minimum(scores, cap_ref[:width])
            peak = jnp.max(scores, axis=0, keepdims=True)
            weights = jnp.exp2((scores - peak) * exp2_scale)
            inverse = 1.0 / jnp.sum(weights, axis=0, keepdims=True)
            probs = (weights * inverse).astype(BF16)
            total_ref[low : row + ROWS] += dot(probs, g_ref[row : row + ROWS, lanes], PLAIN)
    parts = out_ref.shape[0]
    part = length // parts
    for p in range(parts):
        out_ref[p, :part] = total_ref[p * part : (p + 1) * part].astype(BF16)
        out_ref[p, part:] = index_ref[...]


def value_grads(doc_ids, queries, key_states, out_grads, index_rows, parts):
    length = key_states.shape[0]
    part = length // parts
    return pl.pallas_call(
        grads_kernel,
        out_shape=jax.ShapeDtypeStruct((parts, part + index_rows.shape[0], HEAD_DIM), BF16),
        scratch_shapes=[pltpu.VMEM((SPAN + ROWS, ROWS), F32), pltpu.VMEM((length, HEAD_DIM), F32)],
        compiler_params=pltpu.CompilerParams(vmem_limit_bytes=40 * MIB),
    )(doc_ids, queries, key_states, out_grads, index_rows)


def encode_kernel(own_ref, other_ref, hid_own_ref, hid_other_ref, high_ref, low_ref, kept_ref, wave_ref, hid_ref):
    heads = own_ref.shape[0]
    part = other_ref.shape[1]
    half = hid_own_ref.shape[1] // 2
    hid_ref[:part] = hid_own_ref[...]
    hid_ref[part:] = hid_other_ref[...]
    both = 2 * part
    for h in range(heads):
        values = jnp.concatenate([own_ref[h, :part], other_ref[h]], axis=0)
        wave = dot(high_ref[...], values, LAST) + dot(low_ref[...], values, LAST)
        high = wave.astype(BF16)
        wave_ref[h, :, :both] = high
        wave_ref[h, :, both:] = (wave - high.astype(F32)).astype(BF16)

    def step(c, carry):
        at = pl.multiple_of(c * 128, 128)
        rows = jnp.concatenate([hid_ref[:, pl.ds(at, 128)], hid_ref[:, pl.ds(half + at, 128)]], axis=1)
        rows = jnp.concatenate([rows, rows], axis=0)
        for h in range(heads):
            coeffs = dot(wave_ref[h], rows, PLAIN)
            place = pl.multiple_of(part + c * 16, 16)
            index = own_ref[h, pl.ds(place, 16), :].astype(F32).astype(jnp.int32)
            kept = []
            for side in range(2):
                mine = index[side * 8 : side * 8 + 8]
                block, within = mine // 8, mine % 8
                found = jnp.zeros((8, 128), F32)
                for v in range(16):
                    vreg = coeffs[v * 8 : v * 8 + 8, side * 128 : side * 128 + 128]
                    picked = jnp.take_along_axis(vreg, within, axis=0)
                    found = jnp.where(block == v, picked, found)
                kept.append(found)
            kept_ref[h, :, pl.ds(at, 128)] = jnp.concatenate(kept, axis=0).astype(BF16)
        return carry

    lax.fori_loop(0, half // 128, step, 0)


def encode(own, other, hid_own, hid_other, high, low):
    heads, part = own.shape[0], other.shape[1]
    half = hid_own.shape[1] // 2
    return pl.pallas_call(
        encode_kernel,
        out_shape=jax.ShapeDtypeStruct((heads, 2 * KEEP, half), BF16),
        scratch_shapes=[pltpu.VMEM((heads, HEAD_DIM, 4 * part), BF16), pltpu.VMEM((2 * part, 2 * half), BF16)],
        compiler_params=pltpu.CompilerParams(vmem_limit_bytes=40 * MIB),
    )(own, other, hid_own, hid_other, high, low)


def update_kernel(scale, kept_ref, index_ref, high_ref, low_ref, momentum_ref, weight_ref, new_weight_ref, new_momentum_ref):
    frequency = lax.broadcasted_iota(jnp.int32, (HEAD_DIM, 128), 0)
    for c in range(index_ref.shape[1] // 128):
        lanes = slice(c * 128, (c + 1) * 128)
        dense = jnp.zeros((HEAD_DIM, 128), F32)
        for t in range(KEEP):
            dense = jnp.where(frequency == index_ref[t : t + 1, lanes], kept_ref[0, t : t + 1, lanes] * scale, dense)
        high = dense.astype(BF16)
        low = (dense - high.astype(F32)).astype(BF16)
        delta = dot(high, high_ref[...], FIRST) + dot(low, high_ref[...], FIRST) + dot(high, low_ref[...], FIRST)
        fresh = momentum_beta * momentum_ref[lanes] + delta
        new_momentum_ref[lanes] = fresh
        new_weight_ref[lanes] = (
            weight_ref[lanes].astype(F32) - outer_rate * (delta + momentum_beta * fresh)
        ).astype(BF16)


def update(scale, kept, index, high, low, momentum, weight):
    rows = momentum.shape[0]
    block = rows // 4
    table = pl.BlockSpec((HEAD_DIM, HEAD_DIM), lambda i: (0, 0))
    wide = pl.BlockSpec((block, HEAD_DIM), lambda i: (i, 0))
    return pl.pallas_call(
        functools.partial(update_kernel, scale),
        grid=(4,),
        out_shape=(jax.ShapeDtypeStruct(weight.shape, BF16), jax.ShapeDtypeStruct(momentum.shape, F32)),
        in_specs=[
            pl.BlockSpec((1, KEEP, block), lambda i: (i, 0, 0)),
            pl.BlockSpec((KEEP, block), lambda i: (0, i)),
            table,
            table,
            wide,
            wide,
        ],
        out_specs=(wide, wide),
        compiler_params=pltpu.CompilerParams(vmem_limit_bytes=40 * MIB),
    )(kept, index, high, low, momentum, weight)


def swap(x):
    return lax.ppermute(x, "core", [(0, 1), (1, 0)])


def local(hidden_rows, queries, key_states, out_grads, doc_ids, value_weight, momentum, keep_index):
    high, low = dct_tables()
    tensor, ring = ("x", "y_lo"), ("z", "y_hi")
    parts = lax.axis_size(tensor)
    islands = lax.axis_size(ring) * 2
    core = lax.axis_index("core")
    hidden = hidden_rows[0]
    half = hidden.shape[1] // 2
    hid_own = lax.dynamic_slice_in_dim(hidden, core * half, half, 1)
    hid_other = swap(lax.dynamic_slice_in_dim(hidden, (1 - core) * half, half, 1))
    index = keep_index[:, 0, :].T
    mine = lax.dynamic_slice_in_dim(index, core * half, half, 1)
    index_rows = mine.reshape(KEEP, 2, half // 256, 128).transpose(2, 1, 0, 3).reshape(-1, 128).astype(BF16)
    packed = value_grads(doc_ids, queries[0], key_states[0], out_grads[0], index_rows, parts)
    packed = lax.all_to_all(packed, tensor, 0, 0, tiled=True)
    part = hidden.shape[0]
    other = swap(packed[:, :part])
    kept = encode(packed, other, hid_own, hid_other, high, low)
    kept = lax.all_to_all(kept, tensor, 0, 0, tiled=True)
    kept = jnp.sum(kept.astype(F32), axis=0).astype(BF16)
    spread = jnp.broadcast_to(kept[None], (lax.axis_size(ring),) + kept.shape)
    kept = jnp.sum(lax.all_to_all(spread, ring, 0, 0, tiled=True).astype(F32), axis=0)
    there = swap(kept)
    first = jnp.where(core == 0, kept, there)
    second = jnp.where(core == 0, there, kept)
    kept = jnp.concatenate([first, second], axis=0).reshape(4, KEEP, half // 2)
    return update(inner_rate / islands, kept, index, high, low, momentum, value_weight)


def solution(mesh):
    fine = Mesh(mesh.devices.reshape(-1, 2, 2, 4, 2), ("z", "y_hi", "core", "x", "y_lo"))
    island, tensor = ("z", "y_hi", "core"), ("x", "y_lo")
    in_specs = (
        P(island, tensor, None),
        P(island, None, tensor),
        P(island, None, tensor),
        P(island, None, tensor),
        P(island, None),
        P(None, tensor),
        P(None, tensor),
        P(None, tensor, None),
    )
    out_specs = (P(None, tensor), P(None, tensor))
    return jax.shard_map(local, mesh=fine, in_specs=in_specs, out_specs=out_specs, check_vma=False)
```

```python
import functools
import math

import jax
import jax.numpy as jnp
import numpy as np
from jax import lax
from jax.experimental import pallas as pl
from jax.experimental.pallas import tpu as pltpu
from jax.sharding import Mesh
from jax.sharding import PartitionSpec as P

HEAD_DIM = 128
KEEP = 8
SPAN = 512
ROWS = 128
FETCH = 256
STORE = 512

inner_rate = 0.01
outer_rate = 0.7
momentum_beta = 0.9
masked_score = -1e30
exp2_scale = HEAD_DIM ** (-0.5) / math.log(2.0)

BF16 = jnp.bfloat16
F32 = jnp.float32
LAST = (((1,), (1,)), ((), ()))
PLAIN = (((1,), (0,)), ((), ()))
FIRST = (((0,), (0,)), ((), ()))
MIB = 1 << 20


def dot(a, b, dims):
    return lax.dot_general(a, b, dims, preferred_element_type=F32)


def dct_tables():
    frequency = np.arange(HEAD_DIM, dtype=np.float64)[:, None]
    sample = np.arange(HEAD_DIM, dtype=np.float64)[None, :]
    basis = np.cos(np.pi * (sample + 0.5) * frequency / HEAD_DIM)
    table = basis * np.where(frequency == 0.0, math.sqrt(1.0 / HEAD_DIM), math.sqrt(2.0 / HEAD_DIM))
    high = table.astype(jnp.bfloat16)
    low = (table - high.astype(np.float64)).astype(jnp.bfloat16)
    return high, low


def grads_kernel(
    core_ref, doc_hbm, q_hbm, k_hbm, g_hbm, index_hbm, out_ref, doc_ref, q_ref, k_ref, g_ref, index_ref, cap_ref, total_ref, sems
):
    length = k_ref.shape[0]
    group = q_ref.shape[1] // HEAD_DIM
    half = index_ref.shape[1]
    count = length // FETCH

    def fetch(source, target, sem):
        copy = pltpu.make_async_copy(source, target, sems.at[sem])
        copy.start()
        return copy

    doc_copy = fetch(doc_hbm, doc_ref, 0)
    copies = []
    for b in range(count):
        rows = pl.ds(b * FETCH, FETCH)
        copies.append(
            [
                fetch(source.at[rows], target.at[rows], 2 + 3 * b + n)
                for n, (source, target) in enumerate(((k_hbm, k_ref), (q_hbm, q_ref), (g_hbm, g_ref)))
            ]
        )
    at = pl.multiple_of(core_ref[0] * half, 128)
    index_copy = fetch(index_hbm.at[:, pl.ds(at, half)], index_ref, 1)

    total_ref[...] = jnp.zeros_like(total_ref)
    doc_copy.wait()
    docs = doc_ref[...]
    first = jnp.zeros_like(docs)
    for ident in (1, 2, 3):
        before = jnp.sum((docs < ident).astype(jnp.int32), axis=1, keepdims=True)
        first = jnp.where(docs == ident, before, first)
    for row in range(0, length, ROWS):
        if row % FETCH == 0:
            for copy in copies[row // FETCH]:
                copy.wait()
        low = max(0, row - SPAN)
        width = row + ROWS - low
        start = first[:, row : row + ROWS]
        key = lax.broadcasted_iota(jnp.int32, (width, ROWS), 0) + low
        query = lax.broadcasted_iota(jnp.int32, (width, ROWS), 1) + row
        allowed = (key >= start) & (key <= query)
        cap_ref[:width] = jnp.where(allowed, jnp.finfo(F32).max, masked_score)
        for head in range(group):
            lanes = slice(head * HEAD_DIM, (head + 1) * HEAD_DIM)
            scores = dot(k_ref[low : row + ROWS], q_ref[row : row + ROWS, lanes], LAST)
            scores = jnp.minimum(scores, cap_ref[:width])
            peak = jnp.max(scores, axis=0, keepdims=True)
            weights = jnp.exp2((scores - peak) * exp2_scale)
            inverse = 1.0 / jnp.sum(weights, axis=0, keepdims=True)
            probs = (weights * inverse).astype(BF16)
            total_ref[low : row + ROWS] += dot(probs, g_ref[row : row + ROWS, lanes], PLAIN)
    index_copy.wait()
    pieces = []
    for c in range(half // 256):
        for side in range(2):
            lane = side * (half // 2) + c * 128
            pieces.append(index_ref[:, lane : lane + 128])
    index = jnp.concatenate(pieces, axis=0).astype(F32).astype(BF16)
    parts = out_ref.shape[0]
    part = length // parts
    for p in range(parts):
        out_ref[p, :part] = total_ref[p * part : (p + 1) * part].astype(BF16)
        out_ref[p, part:] = index


def in_hbm(*arrays):
    return [pltpu.with_memory_space_constraint(x, pltpu.HBM) for x in arrays]


def in_vmem(*arrays):
    return [pltpu.with_memory_space_constraint(x, pltpu.VMEM) for x in arrays]


HBM = pl.BlockSpec(memory_space=pltpu.HBM)
VMEM = pl.BlockSpec(memory_space=pltpu.VMEM)
SMEM = pl.BlockSpec(memory_space=pltpu.SMEM)


def value_grads(core, doc_ids, queries, key_states, out_grads, index, parts):
    length = key_states.shape[0]
    part = length // parts
    half = index.shape[1] // 2
    index_rows = half * KEEP // 128
    return pl.pallas_call(
        grads_kernel,
        out_shape=jax.ShapeDtypeStruct((parts, part + index_rows, HEAD_DIM), BF16),
        in_specs=[SMEM] + [HBM] * 5,
        out_specs=VMEM,
        scratch_shapes=[
            pltpu.VMEM(doc_ids.shape, jnp.int32),
            pltpu.VMEM(queries.shape, BF16),
            pltpu.VMEM(key_states.shape, BF16),
            pltpu.VMEM(out_grads.shape, BF16),
            pltpu.VMEM((KEEP, half), jnp.int32),
            pltpu.VMEM((SPAN + ROWS, ROWS), F32),
            pltpu.VMEM((length, HEAD_DIM), F32),
            pltpu.SemaphoreType.DMA((2 + 3 * (length // FETCH),)),
        ],
        compiler_params=pltpu.CompilerParams(vmem_limit_bytes=40 * MIB),
    )(core, *in_hbm(doc_ids, queries, key_states, out_grads, index))


def encode_kernel(core_ref, own_ref, other_ref, hid_own_ref, hid_other_ref, high_ref, low_ref, kept_ref, wave_ref):
    heads = own_ref.shape[0]
    part = other_ref.shape[1]
    both = 2 * part
    quarter = hid_own_ref.shape[1] // 4
    for h in range(heads):
        values = jnp.concatenate([own_ref[h, :part], other_ref[h]], axis=0)
        wave = dot(high_ref[...], values, LAST) + dot(low_ref[...], values, LAST)
        high = wave.astype(BF16)
        wave_ref[h, :, :both] = high
        wave_ref[h, :, both:] = (wave - high.astype(F32)).astype(BF16)
    for c in range(quarter // 128):
        first, second = (
            pl.ds(pl.multiple_of(core_ref[0] * (2 * quarter) + side * quarter + c * 128, 128), 128) for side in range(2)
        )
        rows = [jnp.concatenate([ref[:, first], ref[:, second]], axis=1) for ref in (hid_own_ref, hid_other_ref)]
        rows = jnp.concatenate(rows + rows, axis=0)
        for h in range(heads):
            coeffs = dot(wave_ref[h], rows, PLAIN)
            index = own_ref[h, part + c * 16 : part + (c + 1) * 16].astype(F32).astype(jnp.int32)
            kept = []
            for side in range(2):
                mine = index[side * 8 : side * 8 + 8]
                block, within = mine >> 3, mine & 7
                found = jnp.zeros((8, 128), F32)
                for v in range(HEAD_DIM // 8):
                    piece = coeffs[v * 8 : v * 8 + 8, side * 128 : side * 128 + 128]
                    found = jnp.where(block == v, jnp.take_along_axis(piece, within, axis=0), found)
                kept.append(found)
            kept_ref[h, :, c * 128 : (c + 1) * 128] = jnp.concatenate(kept, axis=0).astype(BF16)


def encode(core, own, other, hid_own, hid_other, high, low):
    heads, part = own.shape[0], other.shape[1]
    return pl.pallas_call(
        encode_kernel,
        out_shape=jax.ShapeDtypeStruct((heads, 2 * KEEP, hid_own.shape[1] // 4), BF16),
        in_specs=[SMEM] + [VMEM] * 6,
        out_specs=VMEM,
        scratch_shapes=[pltpu.VMEM((heads, HEAD_DIM, 4 * part), BF16)],
        compiler_params=pltpu.CompilerParams(vmem_limit_bytes=40 * MIB),
    )(core, *in_vmem(own, other, hid_own, hid_other, high, low))


def spread_kernel(kept_ref, out_ref):
    total = kept_ref[0].astype(F32)
    for n in range(1, kept_ref.shape[0]):
        total += kept_ref[n].astype(F32)
    total = total.astype(BF16)
    for n in range(out_ref.shape[0]):
        out_ref[n] = total


def spread(kept, copies):
    return pl.pallas_call(
        spread_kernel,
        out_shape=jax.ShapeDtypeStruct((copies,) + kept.shape[1:], BF16),
        in_specs=[VMEM],
        out_specs=VMEM,
    )(*in_vmem(kept))


def update_kernel(
    scale,
    core_ref,
    own_ref,
    other_ref,
    index_ref,
    high_ref,
    low_ref,
    momentum_ref,
    weight_ref,
    new_weight_hbm,
    new_momentum_hbm,
    new_weight_ref,
    new_momentum_ref,
    sems,
):
    core = core_ref[0]
    frequency = lax.broadcasted_iota(jnp.int32, (HEAD_DIM, 128), 0).astype(F32).astype(BF16)
    total, quarter = momentum_ref.shape[0], own_ref.shape[1]
    copies = []
    for row in range(0, total, 128):
        rows = slice(row, row + 128)
        lane = row % quarter
        place = (row // quarter) % 2 * KEEP
        half = row // (2 * quarter)
        ours = own_ref[place : place + KEEP, lane : lane + 128]
        theirs = other_ref[place : place + KEEP, lane : lane + 128]
        kept = jnp.where(core == half, ours, theirs) * scale
        kept_high = kept.astype(BF16)
        kept_low = (kept - kept_high.astype(F32)).astype(BF16)
        index = index_ref[:, rows].astype(F32).astype(BF16)
        high = jnp.zeros((HEAD_DIM, 128), BF16)
        low = jnp.zeros((HEAD_DIM, 128), BF16)
        for t in range(KEEP):
            here = frequency == index[t : t + 1]
            high = jnp.where(here, kept_high[t : t + 1], high)
            low = jnp.where(here, kept_low[t : t + 1], low)
        delta = dot(high, high_ref[...], FIRST) + dot(low, high_ref[...], FIRST) + dot(high, low_ref[...], FIRST)
        fresh = momentum_beta * momentum_ref[rows] + delta
        new_momentum_ref[rows] = fresh
        new_weight_ref[rows] = (
            weight_ref[rows].astype(F32) - outer_rate * (delta + momentum_beta * fresh)
        ).astype(BF16)
        if (row + 128) % STORE == 0:
            done = pl.ds(row + 128 - STORE, STORE)
            n = 2 * (row // STORE)
            copies.append(pltpu.make_async_copy(new_momentum_ref.at[done], new_momentum_hbm.at[done], sems.at[n]))
            copies.append(pltpu.make_async_copy(new_weight_ref.at[done], new_weight_hbm.at[done], sems.at[n + 1]))
            copies[-2].start()
            copies[-1].start()
    for copy in copies:
        copy.wait()


def update(scale, core, own, other, index, high, low, momentum, weight):
    return pl.pallas_call(
        functools.partial(update_kernel, scale),
        out_shape=(jax.ShapeDtypeStruct(weight.shape, BF16), jax.ShapeDtypeStruct(momentum.shape, F32)),
        in_specs=[SMEM] + [VMEM] * 7,
        out_specs=(HBM, HBM),
        scratch_shapes=[
            pltpu.VMEM(weight.shape, BF16),
            pltpu.VMEM(momentum.shape, F32),
            pltpu.SemaphoreType.DMA((2 * momentum.shape[0] // STORE,)),
        ],
        compiler_params=pltpu.CompilerParams(vmem_limit_bytes=40 * MIB),
    )(core, *in_vmem(own, other, index, high, low, momentum, weight))


def swap(x):
    return lax.ppermute(x, "core", [(0, 1), (1, 0)])


def local(hidden_rows, queries, key_states, out_grads, doc_ids, value_weight, momentum, keep_index):
    high, low = dct_tables()
    tensor, ring = ("x", "y_lo"), ("z", "y_hi")
    islands = lax.axis_size(ring) * 2
    core = lax.axis_index("core").astype(jnp.int32).reshape(1)
    hid_own = hidden_rows[0]
    hid_other = swap(hid_own)
    part = hid_own.shape[0]
    index = keep_index[:, 0, :].T
    packed = value_grads(core, doc_ids, queries[0], key_states[0], out_grads[0], index, lax.axis_size(tensor))
    packed = lax.all_to_all(packed, tensor, 0, 0, tiled=True)
    other = swap(packed[:, :part])
    kept = encode(core, packed, other, hid_own, hid_other, high, low)
    kept = lax.all_to_all(kept, tensor, 0, 0, tiled=True)
    kept = lax.all_to_all(spread(kept, lax.axis_size(ring)), ring, 0, 0, tiled=True)
    kept = jnp.sum(kept.astype(F32), axis=0)
    return update(inner_rate / islands, core, kept, swap(kept), index, high, low, momentum, value_weight)


def solution(mesh):
    fine = Mesh(mesh.devices.reshape(-1, 2, 2, 4, 2), ("z", "y_hi", "core", "x", "y_lo"))
    island, tensor = ("z", "y_hi", "core"), ("x", "y_lo")
    in_specs = (
        P(island, tensor, None),
        P(island, None, tensor),
        P(island, None, tensor),
        P(island, None, tensor),
        P(island, None),
        P(None, tensor),
        P(None, tensor),
        P(None, tensor, None),
    )
    out_specs = (P(None, tensor), P(None, tensor))
    return jax.shard_map(local, mesh=fine, in_specs=in_specs, out_specs=out_specs, check_vma=False)
```

```python
import functools
import math

import jax
import jax.numpy as jnp
import numpy as np
from jax import lax
from jax.experimental import pallas as pl
from jax.experimental.pallas import tpu as pltpu
from jax.sharding import Mesh
from jax.sharding import PartitionSpec as P

HEAD_DIM = 128
KEEP = 8
SPAN = 512
ROWS = 128
STORE = 512

inner_rate = 0.01
outer_rate = 0.7
momentum_beta = 0.9
masked_score = -1e30
exp2_scale = HEAD_DIM ** (-0.5) / math.log(2.0)

BF16 = jnp.bfloat16
F32 = jnp.float32
LAST = (((1,), (1,)), ((), ()))
PLAIN = (((1,), (0,)), ((), ()))
FIRST = (((0,), (0,)), ((), ()))
MIB = 1 << 20


def dot(a, b, dims):
    return lax.dot_general(a, b, dims, preferred_element_type=F32)


def dct_tables():
    frequency = np.arange(HEAD_DIM, dtype=np.float64)[:, None]
    sample = np.arange(HEAD_DIM, dtype=np.float64)[None, :]
    basis = np.cos(np.pi * (sample + 0.5) * frequency / HEAD_DIM)
    table = basis * np.where(frequency == 0.0, math.sqrt(1.0 / HEAD_DIM), math.sqrt(2.0 / HEAD_DIM))
    high = table.astype(jnp.bfloat16)
    low = (table - high.astype(np.float64)).astype(jnp.bfloat16)
    return np.concatenate([high, low])


def grads_kernel(
    core_ref, doc_hbm, q_hbm, k_hbm, g_hbm, index_hbm, out_ref, doc_ref, q_ref, k_ref, g_ref, index_ref, cap_ref, total_ref, sems
):
    length = k_ref.shape[0]
    group = q_ref.shape[1] // HEAD_DIM
    half = index_ref.shape[1]
    at = pl.multiple_of(core_ref[0] * half, 128)
    copies = [
        pltpu.make_async_copy(source, target, sems.at[n])
        for n, (source, target) in enumerate(
            (
                (doc_hbm, doc_ref),
                (k_hbm, k_ref),
                (q_hbm, q_ref),
                (g_hbm, g_ref),
                (index_hbm.at[:, pl.ds(at, half)], index_ref),
            )
        )
    ]
    for copy in copies:
        copy.start()
    total_ref[...] = jnp.zeros_like(total_ref)
    copies[0].wait()
    docs = doc_ref[...]
    first = jnp.zeros_like(docs)
    for ident in (1, 2, 3):
        before = jnp.sum((docs < ident).astype(jnp.int32), axis=1, keepdims=True)
        first = jnp.where(docs == ident, before, first)
    for copy in copies[1:]:
        copy.wait()
    for row in range(0, length, ROWS):
        low = max(0, row - SPAN)
        width = row + ROWS - low
        start = first[:, row : row + ROWS]
        key = lax.broadcasted_iota(jnp.int32, (width, ROWS), 0) + low
        query = lax.broadcasted_iota(jnp.int32, (width, ROWS), 1) + row
        allowed = (key >= start) & (key <= query)
        cap_ref[:width] = jnp.where(allowed, jnp.finfo(F32).max, masked_score)
        for head in range(group):
            lanes = slice(head * HEAD_DIM, (head + 1) * HEAD_DIM)
            scores = dot(k_ref[low : row + ROWS], q_ref[row : row + ROWS, lanes], LAST)
            scores = jnp.minimum(scores, cap_ref[:width])
            peak = jnp.max(scores, axis=0, keepdims=True)
            weights = jnp.exp2((scores - peak) * exp2_scale)
            inverse = 1.0 / jnp.sum(weights, axis=0, keepdims=True)
            probs = (weights * inverse).astype(BF16)
            total_ref[low : row + ROWS] += dot(probs, g_ref[row : row + ROWS, lanes], PLAIN)
    section = half // 4
    pieces = []
    for quarter in range(2):
        for c in range(section // 128):
            for side in range(2):
                lane = (2 * quarter + side) * section + c * 128
                pieces.append(index_ref[:, lane : lane + 128])
    index = jnp.concatenate(pieces, axis=0).astype(F32).astype(BF16)
    parts = out_ref.shape[0]
    part = length // parts
    for p in range(parts):
        out_ref[p, :part] = total_ref[p * part : (p + 1) * part].astype(BF16)
        out_ref[p, part:] = index


def in_hbm(*arrays):
    return [pltpu.with_memory_space_constraint(x, pltpu.HBM) for x in arrays]


def in_vmem(*arrays):
    return [pltpu.with_memory_space_constraint(x, pltpu.VMEM) for x in arrays]


HBM = pl.BlockSpec(memory_space=pltpu.HBM)
VMEM = pl.BlockSpec(memory_space=pltpu.VMEM)
SMEM = pl.BlockSpec(memory_space=pltpu.SMEM)


def value_grads(core, doc_ids, queries, key_states, out_grads, index, parts):
    length = key_states.shape[0]
    part = length // parts
    half = index.shape[1] // 2
    index_rows = half * KEEP // 128
    return pl.pallas_call(
        grads_kernel,
        out_shape=jax.ShapeDtypeStruct((parts, part + index_rows, HEAD_DIM), BF16),
        in_specs=[SMEM] + [HBM] * 5,
        out_specs=VMEM,
        scratch_shapes=[
            pltpu.VMEM(doc_ids.shape, jnp.int32),
            pltpu.VMEM(queries.shape, BF16),
            pltpu.VMEM(key_states.shape, BF16),
            pltpu.VMEM(out_grads.shape, BF16),
            pltpu.VMEM((KEEP, half), jnp.int32),
            pltpu.VMEM((SPAN + ROWS, ROWS), F32),
            pltpu.VMEM((length, HEAD_DIM), F32),
            pltpu.SemaphoreType.DMA((5,)),
        ],
        compiler_params=pltpu.CompilerParams(vmem_limit_bytes=40 * MIB),
    )(core, *in_hbm(doc_ids, queries, key_states, out_grads, index))


def encode_kernel(
    core_ref, own_ref, other_ref, hid_own_ref, hid_other_ref, table_ref, kept_ref, table_out_ref, wave_ref
):
    table_out_ref[...] = table_ref[...]
    heads = own_ref.shape[0]
    part = other_ref.shape[1]
    both = 2 * part
    half = hid_own_ref.shape[1] // 2
    section = half // 4
    chunks = section // 128
    for h in range(heads):
        values = jnp.concatenate([own_ref[h, :part], other_ref[h]], axis=0)
        wave = dot(table_ref[:HEAD_DIM], values, LAST) + dot(table_ref[HEAD_DIM:], values, LAST)
        high = wave.astype(BF16)
        wave_ref[h, :, :both] = high
        wave_ref[h, :, both:] = (wave - high.astype(F32)).astype(BF16)
    for n in range(2 * chunks):
        quarter, c = divmod(n, chunks)
        at = core_ref[0] * half + quarter * (2 * section) + c * 128
        first, second = (pl.ds(pl.multiple_of(at + side * section, 128), 128) for side in range(2))
        rows = [jnp.concatenate([ref[:, first], ref[:, second]], axis=1) for ref in (hid_own_ref, hid_other_ref)]
        rows = jnp.concatenate(rows + rows, axis=0)
        for h in range(heads):
            coeffs = dot(wave_ref[h], rows, PLAIN)
            index = own_ref[h, part + n * 16 : part + (n + 1) * 16].astype(F32).astype(jnp.int32)
            kept = []
            for side in range(2):
                mine = index[side * 8 : side * 8 + 8]
                block, within = mine >> 3, mine & 7
                found = jnp.zeros((8, 128), F32)
                for v in range(HEAD_DIM // 8):
                    piece = coeffs[v * 8 : v * 8 + 8, side * 128 : side * 128 + 128]
                    found = jnp.where(block == v, jnp.take_along_axis(piece, within, axis=0), found)
                kept.append(found)
            kept_ref[quarter, h, :, c * 128 : (c + 1) * 128] = jnp.concatenate(kept, axis=0).astype(BF16)


def encode(core, own, other, hid_own, hid_other, table):
    heads, part = own.shape[0], other.shape[1]
    return pl.pallas_call(
        encode_kernel,
        out_shape=(
            jax.ShapeDtypeStruct((2, heads, 2 * KEEP, hid_own.shape[1] // 8), BF16),
            jax.ShapeDtypeStruct(table.shape, BF16),
        ),
        in_specs=[SMEM] + [VMEM] * 5,
        out_specs=(VMEM, VMEM),
        scratch_shapes=[pltpu.VMEM((heads, HEAD_DIM, 4 * part), BF16)],
        compiler_params=pltpu.CompilerParams(vmem_limit_bytes=40 * MIB),
    )(core, *in_vmem(own, other, hid_own, hid_other, table))


def spread(kept, copies):
    total = jnp.sum(kept.astype(F32), axis=0).astype(BF16)
    return jnp.broadcast_to(total[None], (copies,) + total.shape)


def update_kernel(
    scale,
    core_ref,
    own_ref,
    other_ref,
    index_ref,
    table_ref,
    momentum_ref,
    weight_ref,
    new_weight_hbm,
    new_momentum_hbm,
    new_weight_ref,
    new_momentum_ref,
    sems,
):
    core = core_ref[0]
    frequency = lax.broadcasted_iota(jnp.int32, (HEAD_DIM, 128), 0).astype(F32).astype(BF16)
    high_table, low_table = table_ref[:HEAD_DIM], table_ref[HEAD_DIM:]
    total, section = momentum_ref.shape[0], own_ref.shape[2]
    copies = []
    for row in range(0, total, 128):
        rows = slice(row, row + 128)
        lane = row % section
        place = row // section % 2 * KEEP
        quarter = row // (2 * section) % 2
        half = row // (4 * section)
        ours = own_ref[quarter, place : place + KEEP, lane : lane + 128]
        theirs = other_ref[quarter, place : place + KEEP, lane : lane + 128]
        kept = jnp.where(core == half, ours, theirs) * scale
        kept_high = kept.astype(BF16)
        kept_low = (kept - kept_high.astype(F32)).astype(BF16)
        index = index_ref[:, rows].astype(F32).astype(BF16)
        high = jnp.zeros((HEAD_DIM, 128), BF16)
        low = jnp.zeros((HEAD_DIM, 128), BF16)
        for t in range(KEEP):
            here = frequency == index[t : t + 1]
            high = jnp.where(here, kept_high[t : t + 1], high)
            low = jnp.where(here, kept_low[t : t + 1], low)
        delta = dot(high, high_table, FIRST) + dot(low, high_table, FIRST) + dot(high, low_table, FIRST)
        fresh = momentum_beta * momentum_ref[rows] + delta
        new_momentum_ref[rows] = fresh
        new_weight_ref[rows] = (
            weight_ref[rows].astype(F32) - outer_rate * (delta + momentum_beta * fresh)
        ).astype(BF16)
        if (row + 128) % STORE == 0:
            done = pl.ds(row + 128 - STORE, STORE)
            n = 2 * (row // STORE)
            copies.append(pltpu.make_async_copy(new_momentum_ref.at[done], new_momentum_hbm.at[done], sems.at[n]))
            copies.append(pltpu.make_async_copy(new_weight_ref.at[done], new_weight_hbm.at[done], sems.at[n + 1]))
            copies[-2].start()
            copies[-1].start()
    for copy in copies:
        copy.wait()


def update(scale, core, own, other, index, table, momentum, weight):
    return pl.pallas_call(
        functools.partial(update_kernel, scale),
        out_shape=(jax.ShapeDtypeStruct(weight.shape, BF16), jax.ShapeDtypeStruct(momentum.shape, F32)),
        in_specs=[SMEM] + [VMEM] * 6,
        out_specs=(HBM, HBM),
        scratch_shapes=[
            pltpu.VMEM(weight.shape, BF16),
            pltpu.VMEM(momentum.shape, F32),
            pltpu.SemaphoreType.DMA((2 * momentum.shape[0] // STORE,)),
        ],
        compiler_params=pltpu.CompilerParams(vmem_limit_bytes=40 * MIB),
    )(core, *in_vmem(own, other, index, table, momentum, weight))


def swap(x):
    return lax.ppermute(x, "core", [(0, 1), (1, 0)])


def local(hidden_rows, queries, key_states, out_grads, doc_ids, value_weight, momentum, keep_index):
    tensor, plane, ring = ("x", "y_lo"), ("y_hi", "x", "y_lo"), ("z", "y_hi")
    islands = lax.axis_size(ring) * 2
    core = lax.axis_index("core").astype(jnp.int32).reshape(1)
    hid_own = hidden_rows[0]
    hid_other = swap(hid_own)
    part = hid_own.shape[0]
    index = keep_index[:, 0, :].T
    packed = value_grads(core, doc_ids, queries[0], key_states[0], out_grads[0], index, lax.axis_size(tensor))
    packed = lax.all_to_all(packed, tensor, 0, 0, tiled=True)
    other = swap(packed[:, :part])
    kept, table = encode(core, packed, other, hid_own, hid_other, dct_tables())
    kept = kept.reshape((-1,) + kept.shape[2:])
    kept = lax.all_to_all(kept, plane, 0, 0, tiled=True)
    kept = lax.all_to_all(spread(kept, lax.axis_size(ring)), ring, 0, 0, tiled=True)
    kept = jnp.sum(kept.reshape((lax.axis_size("z"), -1) + kept.shape[1:]).astype(F32), axis=0)
    return update(inner_rate / islands, core, kept, swap(kept), index, table, momentum, value_weight)


def solution(mesh):
    fine = Mesh(mesh.devices.reshape(-1, 2, 2, 4, 2), ("z", "y_hi", "core", "x", "y_lo"))
    island, tensor = ("z", "y_hi", "core"), ("x", "y_lo")
    in_specs = (
        P(island, tensor, None),
        P(island, None, tensor),
        P(island, None, tensor),
        P(island, None, tensor),
        P(island, None),
        P(None, tensor),
        P(None, tensor),
        P(None, tensor, None),
    )
    out_specs = (P(None, tensor), P(None, tensor))
    return jax.shard_map(local, mesh=fine, in_specs=in_specs, out_specs=out_specs, check_vma=False)
```

```python
import functools
import math

import jax
import jax.numpy as jnp
import numpy as np
from jax import lax
from jax.experimental import pallas as pl
from jax.experimental.pallas import tpu as pltpu
from jax.sharding import Mesh
from jax.sharding import PartitionSpec as P

HEAD_DIM = 128
KEEP = 8
SPAN = 512
ROWS = 128
STORE = 512

inner_rate = 0.01
outer_rate = 0.7
momentum_beta = 0.9
masked_score = -1e30
exp2_scale = HEAD_DIM ** (-0.5) / math.log(2.0)

BF16 = jnp.bfloat16
F32 = jnp.float32
LAST = (((1,), (1,)), ((), ()))
PLAIN = (((1,), (0,)), ((), ()))
FIRST = (((0,), (0,)), ((), ()))
MIB = 1 << 20


def dot(a, b, dims):
    return lax.dot_general(a, b, dims, preferred_element_type=F32)


def dct_tables():
    frequency = np.arange(HEAD_DIM, dtype=np.float64)[:, None]
    sample = np.arange(HEAD_DIM, dtype=np.float64)[None, :]
    basis = np.cos(np.pi * (sample + 0.5) * frequency / HEAD_DIM)
    table = basis * np.where(frequency == 0.0, math.sqrt(1.0 / HEAD_DIM), math.sqrt(2.0 / HEAD_DIM))
    high = table.astype(jnp.bfloat16)
    low = (table - high.astype(np.float64)).astype(jnp.bfloat16)
    return np.concatenate([high, low])


def grads_kernel(
    core_ref, doc_hbm, q_hbm, k_hbm, g_hbm, index_hbm, out_ref, doc_ref, q_ref, k_ref, g_ref, index_ref, cap_ref, total_ref, sems
):
    length = k_ref.shape[0]
    group = q_ref.shape[1] // HEAD_DIM
    half = index_ref.shape[1]
    at = pl.multiple_of(core_ref[0] * half, 128)
    copies = [
        pltpu.make_async_copy(source, target, sems.at[n])
        for n, (source, target) in enumerate(
            (
                (doc_hbm, doc_ref),
                (k_hbm, k_ref),
                (q_hbm, q_ref),
                (g_hbm, g_ref),
                (index_hbm.at[:, pl.ds(at, half)], index_ref),
            )
        )
    ]
    for copy in copies:
        copy.start()
    total_ref[...] = jnp.zeros_like(total_ref)
    copies[0].wait()
    docs = doc_ref[...]
    first = jnp.zeros_like(docs)
    for ident in (1, 2, 3):
        before = jnp.sum((docs < ident).astype(jnp.int32), axis=1, keepdims=True)
        first = jnp.where(docs == ident, before, first)
    copies[1].wait()
    copies[2].wait()
    for row in range(0, length, ROWS):
        low = max(0, row - SPAN)
        width = row + ROWS - low
        start = first[:, row : row + ROWS]
        key = lax.broadcasted_iota(jnp.int32, (width, ROWS), 0) + low
        query = lax.broadcasted_iota(jnp.int32, (width, ROWS), 1) + row
        allowed = (key >= start) & (key <= query)
        cap_ref[:width] = jnp.where(allowed, jnp.finfo(F32).max, masked_score)
        for head in range(group):
            lanes = slice(head * HEAD_DIM, (head + 1) * HEAD_DIM)
            scores = dot(k_ref[low : row + ROWS], q_ref[row : row + ROWS, lanes], LAST)
            scores = jnp.minimum(scores, cap_ref[:width])
            peak = jnp.max(scores, axis=0, keepdims=True)
            weights = jnp.exp2((scores - peak) * exp2_scale)
            inverse = 1.0 / jnp.sum(weights, axis=0, keepdims=True)
            probs = (weights * inverse).astype(BF16)
            if row == 0 and head == 0:
                copies[3].wait()
            total_ref[low : row + ROWS] += dot(probs, g_ref[row : row + ROWS, lanes], PLAIN)
    copies[4].wait()
    section = half // 4
    pieces = []
    for quarter in range(2):
        for c in range(section // 128):
            for side in range(2):
                lane = (2 * quarter + side) * section + c * 128
                pieces.append(index_ref[:, lane : lane + 128])
    index = jnp.concatenate(pieces, axis=0).astype(F32).astype(BF16)
    parts = out_ref.shape[0]
    part = length // parts
    for p in range(parts):
        out_ref[p, :part] = total_ref[p * part : (p + 1) * part].astype(BF16)
        out_ref[p, part:] = index


def in_hbm(*arrays):
    return [pltpu.with_memory_space_constraint(x, pltpu.HBM) for x in arrays]


def in_vmem(*arrays):
    return [pltpu.with_memory_space_constraint(x, pltpu.VMEM) for x in arrays]


HBM = pl.BlockSpec(memory_space=pltpu.HBM)
VMEM = pl.BlockSpec(memory_space=pltpu.VMEM)
SMEM = pl.BlockSpec(memory_space=pltpu.SMEM)


def value_grads(core, doc_ids, queries, key_states, out_grads, index, parts):
    length = key_states.shape[0]
    part = length // parts
    half = index.shape[1] // 2
    index_rows = half * KEEP // 128
    return pl.pallas_call(
        grads_kernel,
        out_shape=jax.ShapeDtypeStruct((parts, part + index_rows, HEAD_DIM), BF16),
        in_specs=[SMEM] + [HBM] * 5,
        out_specs=VMEM,
        scratch_shapes=[
            pltpu.VMEM(doc_ids.shape, jnp.int32),
            pltpu.VMEM(queries.shape, BF16),
            pltpu.VMEM(key_states.shape, BF16),
            pltpu.VMEM(out_grads.shape, BF16),
            pltpu.VMEM((KEEP, half), jnp.int32),
            pltpu.VMEM((SPAN + ROWS, ROWS), F32),
            pltpu.VMEM((length, HEAD_DIM), F32),
            pltpu.SemaphoreType.DMA((5,)),
        ],
        compiler_params=pltpu.CompilerParams(vmem_limit_bytes=40 * MIB),
    )(core, *in_hbm(doc_ids, queries, key_states, out_grads, index))


def encode_kernel(
    core_ref,
    own_ref,
    other_ref,
    hid_own_ref,
    hid_other_ref,
    table_ref,
    weight_hbm,
    kept_ref,
    table_out_ref,
    weight_ref,
    wave_ref,
    sems,
):
    copy = pltpu.make_async_copy(weight_hbm, weight_ref, sems.at[0])
    copy.start()
    table_out_ref[...] = table_ref[...]
    heads = own_ref.shape[0]
    part = other_ref.shape[1]
    half = hid_own_ref.shape[1] // 2
    section = half // 4
    chunks = section // 128
    for h in range(heads):
        values = jnp.concatenate([own_ref[h, :part], other_ref[h]], axis=0)
        wave = dot(table_ref[:HEAD_DIM], values, LAST) + dot(table_ref[HEAD_DIM:], values, LAST)
        wave_ref[h] = wave.astype(BF16)
    for n in range(2 * chunks):
        quarter, c = divmod(n, chunks)
        at = core_ref[0] * half + quarter * (2 * section) + c * 128
        first, second = (pl.ds(pl.multiple_of(at + side * section, 128), 128) for side in range(2))
        rows = [jnp.concatenate([ref[:, first], ref[:, second]], axis=1) for ref in (hid_own_ref, hid_other_ref)]
        rows = jnp.concatenate(rows, axis=0)
        for h in range(heads):
            coeffs = dot(wave_ref[h], rows, PLAIN)
            index = own_ref[h, part + n * 16 : part + (n + 1) * 16].astype(F32).astype(jnp.int32)
            kept = []
            for side in range(2):
                mine = index[side * 8 : side * 8 + 8]
                block, within = mine >> 3, mine & 7
                found = jnp.zeros((8, 128), F32)
                for v in range(HEAD_DIM // 8):
                    piece = coeffs[v * 8 : v * 8 + 8, side * 128 : side * 128 + 128]
                    found = jnp.where(block == v, jnp.take_along_axis(piece, within, axis=0), found)
                kept.append(found)
            kept_ref[quarter, h, :, c * 128 : (c + 1) * 128] = jnp.concatenate(kept, axis=0).astype(BF16)
    copy.wait()


def encode(core, own, other, hid_own, hid_other, table, weight):
    heads, part = own.shape[0], other.shape[1]
    return pl.pallas_call(
        encode_kernel,
        out_shape=(
            jax.ShapeDtypeStruct((2, heads, 2 * KEEP, hid_own.shape[1] // 8), BF16),
            jax.ShapeDtypeStruct(table.shape, BF16),
            jax.ShapeDtypeStruct(weight.shape, BF16),
        ),
        in_specs=[SMEM] + [VMEM] * 5 + [HBM],
        out_specs=(VMEM, VMEM, VMEM),
        scratch_shapes=[pltpu.VMEM((heads, HEAD_DIM, 2 * part), BF16), pltpu.SemaphoreType.DMA((1,))],
        compiler_params=pltpu.CompilerParams(vmem_limit_bytes=40 * MIB),
    )(core, *in_vmem(own, other, hid_own, hid_other, table), *in_hbm(weight))


def spread(kept, copies):
    total = jnp.sum(kept.astype(F32), axis=0).astype(BF16)
    return jnp.broadcast_to(total[None], (copies,) + total.shape)


def update_kernel(scale, half_ref, kept_ref, index_ref, table_ref, momentum_ref, weight_ref, *rest):
    new_weight_hbm, new_momentum_hbm, new_weight_ref, new_momentum_ref, sems = rest[-5:]
    frequency = lax.broadcasted_iota(jnp.int32, (HEAD_DIM, 128), 0).astype(F32).astype(BF16)
    high_table, low_table = table_ref[:HEAD_DIM], table_ref[HEAD_DIM:]
    total, section = new_weight_ref.shape[0], kept_ref.shape[2]
    base = half_ref[0] * total
    copies = []
    for row in range(0, total, 128):
        rows = slice(row, row + 128)
        there = pl.ds(pl.multiple_of(base + row, 128), 128)
        lane = row % section
        place = row // section % 2 * KEEP
        kept = kept_ref[row // (2 * section), place : place + KEEP, lane : lane + 128] * scale
        kept_high = kept.astype(BF16)
        kept_low = (kept - kept_high.astype(F32)).astype(BF16)
        index = index_ref[:, there].astype(F32).astype(BF16)
        high = jnp.zeros((HEAD_DIM, 128), BF16)
        low = jnp.zeros((HEAD_DIM, 128), BF16)
        for t in range(KEEP):
            here = frequency == index[t : t + 1]
            high = jnp.where(here, kept_high[t : t + 1], high)
            low = jnp.where(here, kept_low[t : t + 1], low)
        delta = dot(high, high_table, FIRST) + dot(low, high_table, FIRST) + dot(high, low_table, FIRST)
        fresh = momentum_beta * momentum_ref[there] + delta
        new_momentum_ref[rows] = fresh
        new_weight_ref[rows] = (
            weight_ref[there].astype(F32) - outer_rate * (delta + momentum_beta * fresh)
        ).astype(BF16)
        if (row + 128) % STORE == 0:
            done = pl.ds(row + 128 - STORE, STORE)
            target = pl.ds(pl.multiple_of(base + row + 128 - STORE, STORE), STORE)
            n = 2 * (row // STORE)
            copies.append(pltpu.make_async_copy(new_momentum_ref.at[done], new_momentum_hbm.at[target], sems.at[n]))
            copies.append(pltpu.make_async_copy(new_weight_ref.at[done], new_weight_hbm.at[target], sems.at[n + 1]))
            copies[-2].start()
            copies[-1].start()
    for copy in copies:
        copy.wait()


def update(scale, half, kept, index, table, momentum, weight, before=()):
    rows = momentum.shape[0] // 2
    return pl.pallas_call(
        functools.partial(update_kernel, scale),
        out_shape=(jax.ShapeDtypeStruct(weight.shape, BF16), jax.ShapeDtypeStruct(momentum.shape, F32)),
        in_specs=[SMEM] + [VMEM] * 5 + [HBM] * len(before),
        out_specs=(HBM, HBM),
        scratch_shapes=[
            pltpu.VMEM((rows, HEAD_DIM), BF16),
            pltpu.VMEM((rows, HEAD_DIM), F32),
            pltpu.SemaphoreType.DMA((2 * rows // STORE,)),
        ],
        input_output_aliases={6 + n: n for n in range(len(before))},
        compiler_params=pltpu.CompilerParams(vmem_limit_bytes=40 * MIB),
    )(half, *in_vmem(kept, index, table, momentum, weight), *in_hbm(*before))


def swap(x):
    return lax.ppermute(x, "core", [(0, 1), (1, 0)])


def local(hidden_rows, queries, key_states, out_grads, doc_ids, value_weight, momentum, keep_index):
    tensor, plane, ring = ("x", "y_lo"), ("y_hi", "x", "y_lo"), ("z", "y_hi")
    islands = lax.axis_size(ring) * 2
    core = lax.axis_index("core").astype(jnp.int32).reshape(1)
    hid_own = hidden_rows[0]
    hid_other = swap(hid_own)
    part = hid_own.shape[0]
    index = keep_index[:, 0, :].T
    packed = value_grads(core, doc_ids, queries[0], key_states[0], out_grads[0], index, lax.axis_size(tensor))
    packed = lax.all_to_all(packed, tensor, 0, 0, tiled=True)
    other = swap(packed[:, :part])
    kept, table, weight = encode(core, packed, other, hid_own, hid_other, dct_tables(), value_weight)
    kept = kept.reshape((-1,) + kept.shape[2:])
    kept = lax.all_to_all(kept, plane, 0, 0, tiled=True)
    kept = lax.all_to_all(spread(kept, lax.axis_size(ring)), ring, 0, 0, tiled=True)
    kept = jnp.sum(kept.reshape((lax.axis_size("z"), -1) + kept.shape[1:]).astype(F32), axis=0)
    operands = (index, table, momentum, weight)
    before = update(inner_rate / islands, core, kept, *operands)
    return update(inner_rate / islands, 1 - core, swap(kept), *operands, before)


def solution(mesh):
    fine = Mesh(mesh.devices.reshape(-1, 2, 2, 4, 2), ("z", "y_hi", "core", "x", "y_lo"))
    island, tensor = ("z", "y_hi", "core"), ("x", "y_lo")
    in_specs = (
        P(island, tensor, None),
        P(island, None, tensor),
        P(island, None, tensor),
        P(island, None, tensor),
        P(island, None),
        P(None, tensor),
        P(None, tensor),
        P(None, tensor, None),
    )
    out_specs = (P(None, tensor), P(None, tensor))
    return jax.shard_map(local, mesh=fine, in_specs=in_specs, out_specs=out_specs, check_vma=False)
```

```python
import functools
import math

import jax
import jax.numpy as jnp
import numpy as np
from jax import lax
from jax.experimental import pallas as pl
from jax.experimental.pallas import tpu as pltpu
from jax.sharding import Mesh
from jax.sharding import PartitionSpec as P

HEAD_DIM = 128
KEEP = 8
SPAN = 512
ROWS = 128
STORE = 512

inner_rate = 0.01
outer_rate = 0.7
momentum_beta = 0.9
masked_score = -1e30
exp2_scale = HEAD_DIM ** (-0.5) / math.log(2.0)

BF16 = jnp.bfloat16
F32 = jnp.float32
LAST = (((1,), (1,)), ((), ()))
PLAIN = (((1,), (0,)), ((), ()))
FIRST = (((0,), (0,)), ((), ()))
MIB = 1 << 20


def dot(a, b, dims):
    return lax.dot_general(a, b, dims, preferred_element_type=F32)


def dct_tables():
    frequency = np.arange(HEAD_DIM, dtype=np.float64)[:, None]
    sample = np.arange(HEAD_DIM, dtype=np.float64)[None, :]
    basis = np.cos(np.pi * (sample + 0.5) * frequency / HEAD_DIM)
    table = basis * np.where(frequency == 0.0, math.sqrt(1.0 / HEAD_DIM), math.sqrt(2.0 / HEAD_DIM))
    high = table.astype(jnp.bfloat16)
    low = (table - high.astype(np.float64)).astype(jnp.bfloat16)
    return np.concatenate([high, low])


def grads_kernel(
    core_ref, doc_hbm, q_hbm, k_hbm, g_hbm, index_hbm, out_ref, doc_ref, q_ref, k_ref, g_ref, index_ref, cap_ref, total_ref, sems
):
    length = k_ref.shape[0]
    group = q_ref.shape[1] // HEAD_DIM
    half = index_ref.shape[1]
    at = pl.multiple_of(core_ref[0] * half, 128)
    copies = [
        pltpu.make_async_copy(source, target, sems.at[n])
        for n, (source, target) in enumerate(
            (
                (doc_hbm, doc_ref),
                (k_hbm, k_ref),
                (q_hbm, q_ref),
                (g_hbm, g_ref),
                (index_hbm.at[:, pl.ds(at, half)], index_ref),
            )
        )
    ]
    for copy in copies:
        copy.start()
    total_ref[...] = jnp.zeros_like(total_ref)
    copies[0].wait()
    docs = doc_ref[...]
    first = jnp.zeros_like(docs)
    for ident in (1, 2, 3):
        before = jnp.sum((docs < ident).astype(jnp.int32), axis=1, keepdims=True)
        first = jnp.where(docs == ident, before, first)
    copies[1].wait()
    copies[2].wait()
    for row in range(0, length, ROWS):
        low = max(0, row - SPAN)
        width = row + ROWS - low
        start = first[:, row : row + ROWS]
        key = lax.broadcasted_iota(jnp.int32, (width, ROWS), 0) + low
        query = lax.broadcasted_iota(jnp.int32, (width, ROWS), 1) + row
        allowed = (key >= start) & (key <= query)
        cap_ref[:width] = jnp.where(allowed, jnp.finfo(F32).max, masked_score)
        for head in range(group):
            lanes = slice(head * HEAD_DIM, (head + 1) * HEAD_DIM)
            scores = dot(k_ref[low : row + ROWS], q_ref[row : row + ROWS, lanes], LAST)
            scores = jnp.minimum(scores, cap_ref[:width])
            peak = jnp.max(scores, axis=0, keepdims=True)
            weights = jnp.exp2((scores - peak) * exp2_scale)
            inverse = 1.0 / jnp.sum(weights, axis=0, keepdims=True)
            probs = (weights * inverse).astype(BF16)
            if row == 0 and head == 0:
                copies[3].wait()
            total_ref[low : row + ROWS] += dot(probs, g_ref[row : row + ROWS, lanes], PLAIN)
    copies[4].wait()
    section = half // 4
    pieces = []
    for quarter in range(2):
        for c in range(section // 128):
            for side in range(2):
                lane = (2 * quarter + side) * section + c * 128
                pieces.append(index_ref[:, lane : lane + 128])
    index = jnp.concatenate(pieces, axis=0).astype(F32).astype(BF16)
    parts = out_ref.shape[0]
    part = length // parts
    for p in range(parts):
        out_ref[p, :part] = total_ref[p * part : (p + 1) * part].astype(BF16)
        out_ref[p, part:] = index


def in_hbm(*arrays):
    return [pltpu.with_memory_space_constraint(x, pltpu.HBM) for x in arrays]


def in_vmem(*arrays):
    return [pltpu.with_memory_space_constraint(x, pltpu.VMEM) for x in arrays]


HBM = pl.BlockSpec(memory_space=pltpu.HBM)
VMEM = pl.BlockSpec(memory_space=pltpu.VMEM)
SMEM = pl.BlockSpec(memory_space=pltpu.SMEM)


def value_grads(core, doc_ids, queries, key_states, out_grads, index, parts):
    length = key_states.shape[0]
    part = length // parts
    half = index.shape[1] // 2
    index_rows = half * KEEP // 128
    return pl.pallas_call(
        grads_kernel,
        out_shape=jax.ShapeDtypeStruct((parts, part + index_rows, HEAD_DIM), BF16),
        in_specs=[SMEM] + [HBM] * 5,
        out_specs=VMEM,
        scratch_shapes=[
            pltpu.VMEM(doc_ids.shape, jnp.int32),
            pltpu.VMEM(queries.shape, BF16),
            pltpu.VMEM(key_states.shape, BF16),
            pltpu.VMEM(out_grads.shape, BF16),
            pltpu.VMEM((KEEP, half), jnp.int32),
            pltpu.VMEM((SPAN + ROWS, ROWS), F32),
            pltpu.VMEM((length, HEAD_DIM), F32),
            pltpu.SemaphoreType.DMA((5,)),
        ],
        compiler_params=pltpu.CompilerParams(vmem_limit_bytes=16 * MIB),
    )(core, *in_hbm(doc_ids, queries, key_states, out_grads, index))


def encode_kernel(
    core_ref,
    own_ref,
    other_ref,
    hid_own_ref,
    hid_other_ref,
    table_ref,
    kept_ref,
    table_out_ref,
    wave_ref,
):
    table_out_ref[...] = table_ref[...]
    heads = own_ref.shape[0]
    part = other_ref.shape[1]
    half = hid_own_ref.shape[1] // 2
    section = half // 4
    chunks = section // 128
    for h in range(heads):
        values = jnp.concatenate([own_ref[h, :part], other_ref[h]], axis=0)
        wave = dot(table_ref[:HEAD_DIM], values, LAST) + dot(table_ref[HEAD_DIM:], values, LAST)
        wave_ref[h] = wave.astype(BF16)
    for n in range(2 * chunks):
        quarter, c = divmod(n, chunks)
        at = core_ref[0] * half + quarter * (2 * section) + c * 128
        first, second = (pl.ds(pl.multiple_of(at + side * section, 128), 128) for side in range(2))
        rows = [jnp.concatenate([ref[:, first], ref[:, second]], axis=1) for ref in (hid_own_ref, hid_other_ref)]
        rows = jnp.concatenate(rows, axis=0)
        for h in range(heads):
            coeffs = dot(wave_ref[h], rows, PLAIN)
            index = own_ref[h, part + n * 16 : part + (n + 1) * 16].astype(F32).astype(jnp.int32)
            kept = []
            for side in range(2):
                mine = index[side * 8 : side * 8 + 8]
                block, within = mine >> 3, mine & 7
                found = jnp.zeros((8, 128), F32)
                for v in range(HEAD_DIM // 8):
                    piece = coeffs[v * 8 : v * 8 + 8, side * 128 : side * 128 + 128]
                    found = jnp.where(block == v, jnp.take_along_axis(piece, within, axis=0), found)
                kept.append(found)
            kept_ref[quarter, h, :, c * 128 : (c + 1) * 128] = jnp.concatenate(kept, axis=0).astype(BF16)


def encode(core, own, other, hid_own, hid_other, table):
    heads, part = own.shape[0], other.shape[1]
    return pl.pallas_call(
        encode_kernel,
        out_shape=(
            jax.ShapeDtypeStruct((2, heads, 2 * KEEP, hid_own.shape[1] // 8), BF16),
            jax.ShapeDtypeStruct(table.shape, BF16),
        ),
        in_specs=[SMEM] + [VMEM] * 5,
        out_specs=(VMEM, VMEM),
        scratch_shapes=[pltpu.VMEM((heads, HEAD_DIM, 2 * part), BF16)],
        compiler_params=pltpu.CompilerParams(vmem_limit_bytes=16 * MIB),
    )(core, *in_vmem(own, other, hid_own, hid_other, table))


def spread(kept, copies):
    total = lax.optimization_barrier(jnp.sum(kept.astype(F32), axis=0)).astype(BF16)
    return jnp.broadcast_to(total[None], (copies,) + total.shape)


def update_kernel(scale, half_ref, kept_ref, index_ref, table_ref, momentum_ref, weight_ref, *rest):
    new_weight_hbm, new_momentum_hbm, new_weight_ref, new_momentum_ref, sems = rest[-5:]
    frequency = lax.broadcasted_iota(jnp.int32, (HEAD_DIM, 128), 0).astype(F32).astype(BF16)
    high_table, low_table = table_ref[:HEAD_DIM], table_ref[HEAD_DIM:]
    total, section = new_weight_ref.shape[0], kept_ref.shape[2]
    base = half_ref[0] * total
    copies = []
    for row in range(0, total, 128):
        rows = slice(row, row + 128)
        there = pl.ds(pl.multiple_of(base + row, 128), 128)
        lane = row % section
        place = row // section % 2 * KEEP
        kept = kept_ref[row // (2 * section), place : place + KEEP, lane : lane + 128] * scale
        kept_high = kept.astype(BF16)
        kept_low = (kept - kept_high.astype(F32)).astype(BF16)
        index = index_ref[:, there].astype(F32).astype(BF16)
        high = jnp.zeros((HEAD_DIM, 128), BF16)
        low = jnp.zeros((HEAD_DIM, 128), BF16)
        for t in range(KEEP):
            here = frequency == index[t : t + 1]
            high = jnp.where(here, kept_high[t : t + 1], high)
            low = jnp.where(here, kept_low[t : t + 1], low)
        delta = dot(high, high_table, FIRST) + dot(low, high_table, FIRST) + dot(high, low_table, FIRST)
        fresh = momentum_beta * momentum_ref[there] + delta
        new_momentum_ref[rows] = fresh
        new_weight_ref[rows] = (
            weight_ref[there].astype(F32) - outer_rate * (delta + momentum_beta * fresh)
        ).astype(BF16)
        if (row + 128) % STORE == 0:
            done = pl.ds(row + 128 - STORE, STORE)
            target = pl.ds(pl.multiple_of(base + row + 128 - STORE, STORE), STORE)
            n = 2 * (row // STORE)
            copies.append(pltpu.make_async_copy(new_momentum_ref.at[done], new_momentum_hbm.at[target], sems.at[n]))
            copies.append(pltpu.make_async_copy(new_weight_ref.at[done], new_weight_hbm.at[target], sems.at[n + 1]))
            copies[-2].start()
            copies[-1].start()
    for copy in copies:
        copy.wait()


def update(scale, half, kept, index, table, momentum, weight, before=()):
    rows = momentum.shape[0] // 2
    return pl.pallas_call(
        functools.partial(update_kernel, scale),
        out_shape=(jax.ShapeDtypeStruct(weight.shape, BF16), jax.ShapeDtypeStruct(momentum.shape, F32)),
        in_specs=[SMEM] + [VMEM] * 5 + [HBM] * len(before),
        out_specs=(HBM, HBM),
        scratch_shapes=[
            pltpu.VMEM((rows, HEAD_DIM), BF16),
            pltpu.VMEM((rows, HEAD_DIM), F32),
            pltpu.SemaphoreType.DMA((2 * rows // STORE,)),
        ],
        input_output_aliases={6 + n: n for n in range(len(before))},
        compiler_params=pltpu.CompilerParams(vmem_limit_bytes=16 * MIB),
    )(half, *in_vmem(kept, index, table, momentum, weight), *in_hbm(*before))


def swap(x):
    return lax.ppermute(x, "core", [(0, 1), (1, 0)])


def local(hidden_rows, queries, key_states, out_grads, doc_ids, value_weight, momentum, keep_index):
    tensor, plane, ring = ("x", "y_lo"), ("y_hi", "x", "y_lo"), ("z", "y_hi")
    islands = lax.axis_size(ring) * 2
    core = lax.axis_index("core").astype(jnp.int32).reshape(1)
    hid_own = hidden_rows[0]
    hid_other = swap(hid_own)
    part = hid_own.shape[0]
    index = keep_index[:, 0, :].T
    packed = value_grads(core, doc_ids, queries[0], key_states[0], out_grads[0], index, lax.axis_size(tensor))
    packed = lax.all_to_all(packed, tensor, 0, 0, tiled=True)
    other = swap(packed[:, :part])
    kept, table = encode(core, packed, other, hid_own, hid_other, dct_tables())
    kept = kept.reshape((-1,) + kept.shape[2:])
    kept = lax.all_to_all(kept, plane, 0, 0, tiled=True)
    kept = lax.all_to_all(spread(kept, lax.axis_size(ring)), ring, 0, 0, tiled=True)
    kept = jnp.sum(kept.reshape((lax.axis_size("z"), -1) + kept.shape[1:]).astype(F32), axis=0)
    operands = (index, table, momentum, value_weight)
    before = update(inner_rate / islands, core, kept, *operands)
    return update(inner_rate / islands, 1 - core, swap(kept), *operands, before)


def solution(mesh):
    fine = Mesh(mesh.devices.reshape(-1, 2, 2, 4, 2), ("z", "y_hi", "core", "x", "y_lo"))
    island, tensor = ("z", "y_hi", "core"), ("x", "y_lo")
    in_specs = (
        P(island, tensor, None),
        P(island, None, tensor),
        P(island, None, tensor),
        P(island, None, tensor),
        P(island, None),
        P(None, tensor),
        P(None, tensor),
        P(None, tensor, None),
    )
    out_specs = (P(None, tensor), P(None, tensor))
    return jax.shard_map(local, mesh=fine, in_specs=in_specs, out_specs=out_specs, check_vma=False)
```

```python
import functools
import math

import jax
import jax.numpy as jnp
import numpy as np
from jax import lax
from jax.experimental import pallas as pl
from jax.experimental.pallas import tpu as pltpu
from jax.sharding import Mesh
from jax.sharding import PartitionSpec as P

HEAD_DIM = 128
KEEP = 8
SPAN = 512
ROWS = 128
STORE = 512

inner_rate = 0.01
outer_rate = 0.7
momentum_beta = 0.9
masked_score = -1e30
exp2_scale = HEAD_DIM ** (-0.5) / math.log(2.0)

BF16 = jnp.bfloat16
F32 = jnp.float32
LAST = (((1,), (1,)), ((), ()))
PLAIN = (((1,), (0,)), ((), ()))
FIRST = (((0,), (0,)), ((), ()))
MIB = 1 << 20


def dot(a, b, dims):
    return lax.dot_general(a, b, dims, preferred_element_type=F32)


def dct_tables():
    frequency = np.arange(HEAD_DIM, dtype=np.float64)[:, None]
    sample = np.arange(HEAD_DIM, dtype=np.float64)[None, :]
    basis = np.cos(np.pi * (sample + 0.5) * frequency / HEAD_DIM)
    table = basis * np.where(frequency == 0.0, math.sqrt(1.0 / HEAD_DIM), math.sqrt(2.0 / HEAD_DIM))
    high = table.astype(jnp.bfloat16)
    low = (table - high.astype(np.float64)).astype(jnp.bfloat16)
    return np.concatenate([high, low])


def grads_kernel(
    core_ref, doc_hbm, q_hbm, k_hbm, g_hbm, index_hbm, out_ref, doc_ref, q_ref, k_ref, g_ref, index_ref, cap_ref, total_ref, sems
):
    length = k_ref.shape[0]
    group = q_ref.shape[1] // HEAD_DIM
    half = index_ref.shape[1]
    at = pl.multiple_of(core_ref[0] * half, 128)
    copies = [
        pltpu.make_async_copy(source, target, sems.at[n])
        for n, (source, target) in enumerate(
            (
                (doc_hbm, doc_ref),
                (k_hbm, k_ref),
                (q_hbm, q_ref),
                (g_hbm, g_ref),
                (index_hbm.at[:, pl.ds(at, half)], index_ref),
            )
        )
    ]
    for copy in copies:
        copy.start()
    total_ref[...] = jnp.zeros_like(total_ref)
    copies[0].wait()
    docs = doc_ref[...]
    first = jnp.zeros_like(docs)
    for ident in (1, 2, 3):
        before = jnp.sum((docs < ident).astype(jnp.int32), axis=1, keepdims=True)
        first = jnp.where(docs == ident, before, first)
    copies[1].wait()
    copies[2].wait()
    for row in range(0, length, ROWS):
        low = max(0, row - SPAN)
        width = row + ROWS - low
        start = first[:, row : row + ROWS]
        key = lax.broadcasted_iota(jnp.int32, (width, ROWS), 0) + low
        query = lax.broadcasted_iota(jnp.int32, (width, ROWS), 1) + row
        allowed = (key >= start) & (key <= query)
        cap_ref[:width] = jnp.where(allowed, jnp.finfo(F32).max, masked_score)
        for head in range(group):
            lanes = slice(head * HEAD_DIM, (head + 1) * HEAD_DIM)
            scores = dot(k_ref[low : row + ROWS], q_ref[row : row + ROWS, lanes], LAST)
            scores = jnp.minimum(scores, cap_ref[:width])
            peak = jnp.max(scores, axis=0, keepdims=True)
            weights = jnp.exp2((scores - peak) * exp2_scale)
            inverse = 1.0 / jnp.sum(weights, axis=0, keepdims=True)
            probs = (weights * inverse).astype(BF16)
            if row == 0 and head == 0:
                copies[3].wait()
            total_ref[low : row + ROWS] += dot(probs, g_ref[row : row + ROWS, lanes], PLAIN)
    copies[4].wait()
    section = half // 4
    pieces = []
    for quarter in range(2):
        for c in range(section // 128):
            for side in range(2):
                lane = (2 * quarter + side) * section + c * 128
                pieces.append(index_ref[:, lane : lane + 128])
    index = jnp.concatenate(pieces, axis=0).astype(F32).astype(BF16)
    parts = out_ref.shape[0]
    part = length // parts
    for p in range(parts):
        out_ref[p, :part] = total_ref[p * part : (p + 1) * part].astype(BF16)
        out_ref[p, part:] = index


def in_hbm(*arrays):
    return [pltpu.with_memory_space_constraint(x, pltpu.HBM) for x in arrays]


def in_vmem(*arrays):
    return [pltpu.with_memory_space_constraint(x, pltpu.VMEM) for x in arrays]


HBM = pl.BlockSpec(memory_space=pltpu.HBM)
VMEM = pl.BlockSpec(memory_space=pltpu.VMEM)
SMEM = pl.BlockSpec(memory_space=pltpu.SMEM)


def value_grads(core, doc_ids, queries, key_states, out_grads, index, parts):
    length = key_states.shape[0]
    part = length // parts
    half = index.shape[1] // 2
    index_rows = half * KEEP // 128
    return pl.pallas_call(
        grads_kernel,
        out_shape=jax.ShapeDtypeStruct((parts, part + index_rows, HEAD_DIM), BF16),
        in_specs=[SMEM] + [HBM] * 5,
        out_specs=VMEM,
        scratch_shapes=[
            pltpu.VMEM(doc_ids.shape, jnp.int32),
            pltpu.VMEM(queries.shape, BF16),
            pltpu.VMEM(key_states.shape, BF16),
            pltpu.VMEM(out_grads.shape, BF16),
            pltpu.VMEM((KEEP, half), jnp.int32),
            pltpu.VMEM((SPAN + ROWS, ROWS), F32),
            pltpu.VMEM((length, HEAD_DIM), F32),
            pltpu.SemaphoreType.DMA((5,)),
        ],
        compiler_params=pltpu.CompilerParams(vmem_limit_bytes=16 * MIB),
    )(core, *in_hbm(doc_ids, queries, key_states, out_grads, index))


def encode_kernel(
    core_ref,
    own_ref,
    other_ref,
    hid_own_ref,
    hid_other_ref,
    table_ref,
    kept_ref,
    table_out_ref,
    wave_ref,
):
    table_out_ref[...] = table_ref[...]
    heads = own_ref.shape[0]
    part = other_ref.shape[1]
    half = hid_own_ref.shape[1] // 2
    section = half // 4
    chunks = section // 128
    for h in range(heads):
        values = jnp.concatenate([own_ref[h, :part], other_ref[h]], axis=0)
        wave = dot(table_ref[:HEAD_DIM], values, LAST) + dot(table_ref[HEAD_DIM:], values, LAST)
        wave_ref[h] = wave.astype(BF16)
    for n in range(2 * chunks):
        quarter, c = divmod(n, chunks)
        at = core_ref[0] * half + quarter * (2 * section) + c * 128
        first, second = (pl.ds(pl.multiple_of(at + side * section, 128), 128) for side in range(2))
        rows = [jnp.concatenate([ref[:, first], ref[:, second]], axis=1) for ref in (hid_own_ref, hid_other_ref)]
        rows = jnp.concatenate(rows, axis=0)
        for h in range(heads):
            coeffs = dot(wave_ref[h], rows, PLAIN)
            index = own_ref[h, part + n * 16 : part + (n + 1) * 16].astype(F32).astype(jnp.int32)
            kept = []
            for side in range(2):
                mine = index[side * 8 : side * 8 + 8]
                block, within = mine >> 3, mine & 7
                found = jnp.zeros((8, 128), F32)
                for v in range(HEAD_DIM // 8):
                    piece = coeffs[v * 8 : v * 8 + 8, side * 128 : side * 128 + 128]
                    found = jnp.where(block == v, jnp.take_along_axis(piece, within, axis=0), found)
                kept.append(found)
            kept_ref[quarter, h, :, c * 128 : (c + 1) * 128] = jnp.concatenate(kept, axis=0).astype(BF16)


def encode(core, own, other, hid_own, hid_other, table):
    heads, part = own.shape[0], other.shape[1]
    return pl.pallas_call(
        encode_kernel,
        out_shape=(
            jax.ShapeDtypeStruct((2, heads, 2 * KEEP, hid_own.shape[1] // 8), BF16),
            jax.ShapeDtypeStruct(table.shape, BF16),
        ),
        in_specs=[SMEM] + [VMEM] * 5,
        out_specs=(VMEM, VMEM),
        scratch_shapes=[pltpu.VMEM((heads, HEAD_DIM, 2 * part), BF16)],
        compiler_params=pltpu.CompilerParams(vmem_limit_bytes=16 * MIB),
    )(core, *in_vmem(own, other, hid_own, hid_other, table))


def spread(kept, copies):
    total = lax.optimization_barrier(jnp.sum(kept.astype(F32), axis=0)).astype(BF16)
    return jnp.broadcast_to(total[None], (copies,) + total.shape)


def update_rows(scale, base, row, kept_ref, index_ref, table_ref, momentum_ref, weight_ref, new_weight_ref, new_momentum_ref):
    frequency = lax.broadcasted_iota(jnp.int32, (HEAD_DIM, 128), 0).astype(F32).astype(BF16)
    high_table, low_table = table_ref[:HEAD_DIM], table_ref[HEAD_DIM:]
    section = kept_ref.shape[2]
    rows = slice(row, row + 128)
    there = pl.ds(pl.multiple_of(base + row, 128), 128)
    lane = row % section
    place = row // section % 2 * KEEP
    kept = kept_ref[row // (2 * section), place : place + KEEP, lane : lane + 128] * scale
    kept_high = kept.astype(BF16)
    kept_low = (kept - kept_high.astype(F32)).astype(BF16)
    index = index_ref[:, there].astype(F32).astype(BF16)
    high = jnp.zeros((HEAD_DIM, 128), BF16)
    low = jnp.zeros((HEAD_DIM, 128), BF16)
    for t in range(KEEP):
        here = frequency == index[t : t + 1]
        high = jnp.where(here, kept_high[t : t + 1], high)
        low = jnp.where(here, kept_low[t : t + 1], low)
    delta = dot(high, high_table, FIRST) + dot(low, high_table, FIRST) + dot(high, low_table, FIRST)
    fresh = momentum_beta * momentum_ref[there] + delta
    new_momentum_ref[rows] = fresh
    new_weight_ref[rows] = (
        weight_ref[there].astype(F32) - outer_rate * (delta + momentum_beta * fresh)
    ).astype(BF16)


def update_first_kernel(scale, half_ref, *refs):
    total = refs[-1].shape[0]
    for row in range(0, total, 128):
        update_rows(scale, half_ref[0] * total, row, *refs)


def update_second_kernel(scale, half_ref, *refs):
    operands = refs[:5]
    first_weight_ref, first_momentum_ref, weight_hbm, momentum_hbm, new_weight_ref, new_momentum_ref, sems = refs[5:]
    total = new_weight_ref.shape[0]
    half = half_ref[0]
    copies = []

    def store(source, target, base, row, count):
        rows = pl.ds(pl.multiple_of(base + row, STORE), count)
        copies.append(pltpu.make_async_copy(source.at[pl.ds(row, count)], target.at[rows], sems.at[len(copies)]))
        copies[-1].start()

    store(first_momentum_ref, momentum_hbm, (1 - half) * total, 0, total)
    store(first_weight_ref, weight_hbm, (1 - half) * total, 0, total)
    for row in range(0, total, 128):
        update_rows(scale, half * total, row, *operands, new_weight_ref, new_momentum_ref)
        if (row + 128) % STORE == 0:
            store(new_momentum_ref, momentum_hbm, half * total, row + 128 - STORE, STORE)
            store(new_weight_ref, weight_hbm, half * total, row + 128 - STORE, STORE)
    for copy in copies:
        copy.wait()


def update_first(scale, half, kept, index, table, momentum, weight):
    rows = momentum.shape[0] // 2
    return pl.pallas_call(
        functools.partial(update_first_kernel, scale),
        out_shape=(
            jax.ShapeDtypeStruct((rows, HEAD_DIM), BF16),
            jax.ShapeDtypeStruct((rows, HEAD_DIM), F32),
        ),
        in_specs=[SMEM] + [VMEM] * 5,
        out_specs=(VMEM, VMEM),
        compiler_params=pltpu.CompilerParams(vmem_limit_bytes=16 * MIB),
    )(half, *in_vmem(kept, index, table, momentum, weight))


def update_second(scale, half, kept, index, table, momentum, weight, first_weight, first_momentum):
    rows = momentum.shape[0] // 2
    return pl.pallas_call(
        functools.partial(update_second_kernel, scale),
        out_shape=(jax.ShapeDtypeStruct(weight.shape, BF16), jax.ShapeDtypeStruct(momentum.shape, F32)),
        in_specs=[SMEM] + [VMEM] * 7,
        out_specs=(HBM, HBM),
        scratch_shapes=[
            pltpu.VMEM((rows, HEAD_DIM), BF16),
            pltpu.VMEM((rows, HEAD_DIM), F32),
            pltpu.SemaphoreType.DMA((2 + 2 * rows // STORE,)),
        ],
        compiler_params=pltpu.CompilerParams(vmem_limit_bytes=16 * MIB),
    )(half, *in_vmem(kept, index, table, momentum, weight, first_weight, first_momentum))


def swap(x):
    return lax.ppermute(x, "core", [(0, 1), (1, 0)])


def local(hidden_rows, queries, key_states, out_grads, doc_ids, value_weight, momentum, keep_index):
    tensor, near, ring = ("x", "y_lo"), ("z_lo", "x", "y_lo"), ("y_hi", "z_hi", "z_lo")
    islands = lax.axis_size(ring) * 2
    core = lax.axis_index("core").astype(jnp.int32).reshape(1)
    hid_own = hidden_rows[0]
    hid_other = swap(hid_own)
    part = hid_own.shape[0]
    index = keep_index[:, 0, :].T
    packed = value_grads(core, doc_ids, queries[0], key_states[0], out_grads[0], index, lax.axis_size(tensor))
    packed = lax.all_to_all(packed, tensor, 0, 0, tiled=True)
    other = swap(packed[:, :part])
    kept, table = encode(core, packed, other, hid_own, hid_other, dct_tables())
    kept = kept.reshape((-1,) + kept.shape[2:])
    kept = lax.all_to_all(kept, near, 0, 0, tiled=True)
    kept = lax.all_to_all(spread(kept, lax.axis_size(ring)), ring, 0, 0, tiled=True)
    kept = jnp.sum(kept.reshape((-1, lax.axis_size("z_lo")) + kept.shape[1:]).astype(F32), axis=0)
    operands = (index, table, momentum, value_weight)
    first = update_first(inner_rate / islands, core, kept, *operands)
    return update_second(inner_rate / islands, 1 - core, swap(kept), *operands, *first)


def solution(mesh):
    island, tensor = ("z_hi", "z_lo", "y_hi", "core"), ("x", "y_lo")
    fine = Mesh(mesh.devices.reshape(-1, 2, 2, 2, 4, 2), island + tensor)
    in_specs = (
        P(island, tensor, None),
        P(island, None, tensor),
        P(island, None, tensor),
        P(island, None, tensor),
        P(island, None),
        P(None, tensor),
        P(None, tensor),
        P(None, tensor, None),
    )
    out_specs = (P(None, tensor), P(None, tensor))
    return jax.shard_map(local, mesh=fine, in_specs=in_specs, out_specs=out_specs, check_vma=False)
```

```python
import functools
import math

import jax
import jax.numpy as jnp
import numpy as np
from jax import lax
from jax.experimental import pallas as pl
from jax.experimental.pallas import tpu as pltpu
from jax.sharding import Mesh
from jax.sharding import PartitionSpec as P

HEAD_DIM = 128
KEEP = 8
SPAN = 512
ROWS = 128
STORE = 512

inner_rate = 0.01
outer_rate = 0.7
momentum_beta = 0.9
masked_score = -1e30
exp2_scale = HEAD_DIM ** (-0.5) / math.log(2.0)

BF16 = jnp.bfloat16
F32 = jnp.float32
LAST = (((1,), (1,)), ((), ()))
PLAIN = (((1,), (0,)), ((), ()))
FIRST = (((0,), (0,)), ((), ()))
MIB = 1 << 20


def dot(a, b, dims):
    return lax.dot_general(a, b, dims, preferred_element_type=F32)


def dct_tables():
    frequency = np.arange(HEAD_DIM, dtype=np.float64)[:, None]
    sample = np.arange(HEAD_DIM, dtype=np.float64)[None, :]
    basis = np.cos(np.pi * (sample + 0.5) * frequency / HEAD_DIM)
    table = basis * np.where(frequency == 0.0, math.sqrt(1.0 / HEAD_DIM), math.sqrt(2.0 / HEAD_DIM))
    high = table.astype(jnp.bfloat16)
    low = (table - high.astype(np.float64)).astype(jnp.bfloat16)
    return np.concatenate([high, low])


def grads_kernel(
    core_ref, doc_hbm, q_hbm, k_hbm, g_hbm, index_hbm, out_ref, doc_ref, q_ref, k_ref, g_ref, index_ref, cap_ref, total_ref, sems
):
    length = k_ref.shape[0]
    group = q_ref.shape[1] // HEAD_DIM
    half = index_ref.shape[1]
    at = pl.multiple_of(core_ref[0] * half, 128)
    copies = [
        pltpu.make_async_copy(source, target, sems.at[n])
        for n, (source, target) in enumerate(
            (
                (doc_hbm, doc_ref),
                (k_hbm, k_ref),
                (q_hbm, q_ref),
                (g_hbm, g_ref),
                (index_hbm.at[:, pl.ds(at, half)], index_ref),
            )
        )
    ]
    for copy in copies:
        copy.start()
    total_ref[...] = jnp.zeros_like(total_ref)
    copies[0].wait()
    docs = doc_ref[...]
    first = jnp.zeros_like(docs)
    for ident in (1, 2, 3):
        before = jnp.sum((docs < ident).astype(jnp.int32), axis=1, keepdims=True)
        first = jnp.where(docs == ident, before, first)
    copies[1].wait()
    copies[2].wait()
    for row in range(0, length, ROWS):
        low = max(0, row - SPAN)
        width = row + ROWS - low
        start = first[:, row : row + ROWS]
        key = lax.broadcasted_iota(jnp.int32, (width, ROWS), 0) + low
        query = lax.broadcasted_iota(jnp.int32, (width, ROWS), 1) + row
        allowed = (key >= start) & (key <= query)
        cap_ref[:width] = jnp.where(allowed, jnp.finfo(F32).max, masked_score)
        for head in range(group):
            lanes = slice(head * HEAD_DIM, (head + 1) * HEAD_DIM)
            scores = dot(k_ref[low : row + ROWS], q_ref[row : row + ROWS, lanes], LAST)
            scores = jnp.minimum(scores, cap_ref[:width])
            peak = jnp.max(scores, axis=0, keepdims=True)
            weights = jnp.exp2((scores - peak) * exp2_scale)
            inverse = 1.0 / jnp.sum(weights, axis=0, keepdims=True)
            probs = (weights * inverse).astype(BF16)
            if row == 0 and head == 0:
                copies[3].wait()
            total_ref[low : row + ROWS] += dot(probs, g_ref[row : row + ROWS, lanes], PLAIN)
    copies[4].wait()
    section = half // 4
    pieces = []
    for quarter in range(2):
        for c in range(section // 128):
            for side in range(2):
                lane = (2 * quarter + side) * section + c * 128
                pieces.append(index_ref[:, lane : lane + 128])
    index = jnp.concatenate(pieces, axis=0).astype(F32).astype(BF16)
    parts = out_ref.shape[0]
    part = length // parts
    for p in range(parts):
        out_ref[p, :part] = total_ref[p * part : (p + 1) * part].astype(BF16)
        out_ref[p, part:] = index


def in_hbm(*arrays):
    return [pltpu.with_memory_space_constraint(x, pltpu.HBM) for x in arrays]


def in_vmem(*arrays):
    return [pltpu.with_memory_space_constraint(x, pltpu.VMEM) for x in arrays]


HBM = pl.BlockSpec(memory_space=pltpu.HBM)
VMEM = pl.BlockSpec(memory_space=pltpu.VMEM)
SMEM = pl.BlockSpec(memory_space=pltpu.SMEM)


def value_grads(core, doc_ids, queries, key_states, out_grads, index, parts):
    length = key_states.shape[0]
    part = length // parts
    half = index.shape[1] // 2
    index_rows = half * KEEP // 128
    return pl.pallas_call(
        grads_kernel,
        out_shape=jax.ShapeDtypeStruct((parts, part + index_rows, HEAD_DIM), BF16),
        in_specs=[SMEM] + [HBM] * 5,
        out_specs=VMEM,
        scratch_shapes=[
            pltpu.VMEM(doc_ids.shape, jnp.int32),
            pltpu.VMEM(queries.shape, BF16),
            pltpu.VMEM(key_states.shape, BF16),
            pltpu.VMEM(out_grads.shape, BF16),
            pltpu.VMEM((KEEP, half), jnp.int32),
            pltpu.VMEM((SPAN + ROWS, ROWS), F32),
            pltpu.VMEM((length, HEAD_DIM), F32),
            pltpu.SemaphoreType.DMA((5,)),
        ],
        compiler_params=pltpu.CompilerParams(vmem_limit_bytes=16 * MIB),
    )(core, *in_hbm(doc_ids, queries, key_states, out_grads, index))


def encode_kernel(
    core_ref,
    own_ref,
    other_ref,
    hid_own_ref,
    hid_other_ref,
    table_ref,
    kept_ref,
    table_out_ref,
    wave_ref,
):
    table_out_ref[...] = table_ref[...]
    heads = own_ref.shape[0]
    part = other_ref.shape[1]
    half = hid_own_ref.shape[1] // 2
    section = half // 4
    chunks = section // 128
    for h in range(heads):
        values = jnp.concatenate([own_ref[h, :part], other_ref[h]], axis=0)
        wave = dot(table_ref[:HEAD_DIM], values, LAST) + dot(table_ref[HEAD_DIM:], values, LAST)
        wave_ref[h] = wave.astype(BF16)
    for n in range(2 * chunks):
        quarter, c = divmod(n, chunks)
        at = core_ref[0] * half + quarter * (2 * section) + c * 128
        first, second = (pl.ds(pl.multiple_of(at + side * section, 128), 128) for side in range(2))
        rows = [jnp.concatenate([ref[:, first], ref[:, second]], axis=1) for ref in (hid_own_ref, hid_other_ref)]
        rows = jnp.concatenate(rows, axis=0)
        for h in range(heads):
            coeffs = dot(wave_ref[h], rows, PLAIN)
            index = own_ref[h, part + n * 16 : part + (n + 1) * 16].astype(F32).astype(jnp.int32)
            kept = []
            for side in range(2):
                mine = index[side * 8 : side * 8 + 8]
                block, within = mine >> 3, mine & 7
                found = jnp.zeros((8, 128), F32)
                for v in range(HEAD_DIM // 8):
                    piece = coeffs[v * 8 : v * 8 + 8, side * 128 : side * 128 + 128]
                    found = jnp.where(block == v, jnp.take_along_axis(piece, within, axis=0), found)
                kept.append(found)
            kept_ref[h, quarter, :, c * 128 : (c + 1) * 128] = jnp.concatenate(kept, axis=0).astype(BF16)


def encode(core, own, other, hid_own, hid_other, table):
    heads, part = own.shape[0], other.shape[1]
    return pl.pallas_call(
        encode_kernel,
        out_shape=(
            jax.ShapeDtypeStruct((heads, 2, 2 * KEEP, hid_own.shape[1] // 8), BF16),
            jax.ShapeDtypeStruct(table.shape, BF16),
        ),
        in_specs=[SMEM] + [VMEM] * 5,
        out_specs=(VMEM, VMEM),
        scratch_shapes=[pltpu.VMEM((heads, HEAD_DIM, 2 * part), BF16)],
        compiler_params=pltpu.CompilerParams(vmem_limit_bytes=16 * MIB),
    )(core, *in_vmem(own, other, hid_own, hid_other, table))


def spread(kept, copies):
    total = lax.optimization_barrier(jnp.sum(kept.astype(F32), axis=0)).astype(BF16)
    return jnp.broadcast_to(total[None], (copies,) + total.shape)


def update_rows(scale, base, row, kept_ref, index_ref, table_ref, momentum_ref, weight_ref, new_weight_ref, new_momentum_ref):
    frequency = lax.broadcasted_iota(jnp.int32, (HEAD_DIM, 128), 0).astype(F32).astype(BF16)
    high_table, low_table = table_ref[:HEAD_DIM], table_ref[HEAD_DIM:]
    section = kept_ref.shape[2]
    rows = slice(row, row + 128)
    there = pl.ds(pl.multiple_of(base + row, 128), 128)
    lane = row % section
    place = row // section % 2 * KEEP
    kept = kept_ref[row // (2 * section), place : place + KEEP, lane : lane + 128] * scale
    kept_high = kept.astype(BF16)
    kept_low = (kept - kept_high.astype(F32)).astype(BF16)
    index = index_ref[:, there].astype(F32).astype(BF16)
    high = jnp.zeros((HEAD_DIM, 128), BF16)
    low = jnp.zeros((HEAD_DIM, 128), BF16)
    for t in range(KEEP):
        here = frequency == index[t : t + 1]
        high = jnp.where(here, kept_high[t : t + 1], high)
        low = jnp.where(here, kept_low[t : t + 1], low)
    delta = dot(high, high_table, FIRST) + dot(low, high_table, FIRST) + dot(high, low_table, FIRST)
    fresh = momentum_beta * momentum_ref[there] + delta
    new_momentum_ref[rows] = fresh
    new_weight_ref[rows] = (
        weight_ref[there].astype(F32) - outer_rate * (delta + momentum_beta * fresh)
    ).astype(BF16)


def update_first_kernel(scale, half_ref, *refs):
    total = refs[-1].shape[0]
    for row in range(0, total, 128):
        update_rows(scale, half_ref[0] * total, row, *refs)


def update_second_kernel(scale, half_ref, *refs):
    operands = refs[:5]
    first_weight_ref, first_momentum_ref, weight_hbm, momentum_hbm, new_weight_ref, new_momentum_ref, sems = refs[5:]
    total = new_weight_ref.shape[0]
    half = half_ref[0]
    copies = []

    def store(source, target, base, row, count):
        rows = pl.ds(pl.multiple_of(base + row, STORE), count)
        copies.append(pltpu.make_async_copy(source.at[pl.ds(row, count)], target.at[rows], sems.at[len(copies)]))
        copies[-1].start()

    store(first_momentum_ref, momentum_hbm, (1 - half) * total, 0, total)
    store(first_weight_ref, weight_hbm, (1 - half) * total, 0, total)
    for row in range(0, total, 128):
        update_rows(scale, half * total, row, *operands, new_weight_ref, new_momentum_ref)
        if (row + 128) % STORE == 0:
            store(new_momentum_ref, momentum_hbm, half * total, row + 128 - STORE, STORE)
            store(new_weight_ref, weight_hbm, half * total, row + 128 - STORE, STORE)
    for copy in copies:
        copy.wait()


def update_first(scale, half, kept, index, table, momentum, weight):
    rows = momentum.shape[0] // 2
    return pl.pallas_call(
        functools.partial(update_first_kernel, scale),
        out_shape=(
            jax.ShapeDtypeStruct((rows, HEAD_DIM), BF16),
            jax.ShapeDtypeStruct((rows, HEAD_DIM), F32),
        ),
        in_specs=[SMEM] + [VMEM] * 5,
        out_specs=(VMEM, VMEM),
        compiler_params=pltpu.CompilerParams(vmem_limit_bytes=16 * MIB),
    )(half, *in_vmem(kept, index, table, momentum, weight))


def update_second(scale, half, kept, index, table, momentum, weight, first_weight, first_momentum):
    rows = momentum.shape[0] // 2
    return pl.pallas_call(
        functools.partial(update_second_kernel, scale),
        out_shape=(jax.ShapeDtypeStruct(weight.shape, BF16), jax.ShapeDtypeStruct(momentum.shape, F32)),
        in_specs=[SMEM] + [VMEM] * 7,
        out_specs=(HBM, HBM),
        scratch_shapes=[
            pltpu.VMEM((rows, HEAD_DIM), BF16),
            pltpu.VMEM((rows, HEAD_DIM), F32),
            pltpu.SemaphoreType.DMA((2 + 2 * rows // STORE,)),
        ],
        compiler_params=pltpu.CompilerParams(vmem_limit_bytes=16 * MIB),
    )(half, *in_vmem(kept, index, table, momentum, weight, first_weight, first_momentum))


def swap(x):
    return lax.ppermute(x, "core", [(0, 1), (1, 0)])


def local(hidden_rows, queries, key_states, out_grads, doc_ids, value_weight, momentum, keep_index):
    tensor, near, ring = ("x", "y_lo"), ("x", "y_lo", "z_lo"), ("y_hi", "z_hi", "z_lo")
    islands = lax.axis_size(ring) * 2
    core = lax.axis_index("core").astype(jnp.int32).reshape(1)
    hid_own = hidden_rows[0]
    hid_other = swap(hid_own)
    part = hid_own.shape[0]
    index = keep_index[:, 0, :].T
    packed = value_grads(core, doc_ids, queries[0], key_states[0], out_grads[0], index, lax.axis_size(tensor))
    packed = lax.all_to_all(packed, tensor, 0, 0, tiled=True)
    other = swap(packed[:, :part])
    kept, table = encode(core, packed, other, hid_own, hid_other, dct_tables())
    kept = kept.reshape((-1,) + kept.shape[2:])
    kept = lax.all_to_all(kept, near, 0, 0, tiled=True)
    kept = lax.all_to_all(spread(kept, lax.axis_size(ring)), ring, 0, 0, tiled=True)
    kept = jnp.sum(kept.reshape((-1, lax.axis_size("z_lo")) + kept.shape[1:]).astype(F32), axis=0)
    operands = (index, table, momentum, value_weight)
    first = update_first(inner_rate / islands, core, kept, *operands)
    return update_second(inner_rate / islands, 1 - core, swap(kept), *operands, *first)


def solution(mesh):
    island, tensor = ("z_hi", "z_lo", "y_hi", "core"), ("x", "y_lo")
    fine = Mesh(mesh.devices.reshape(-1, 2, 2, 2, 4, 2), island + tensor)
    in_specs = (
        P(island, tensor, None),
        P(island, None, tensor),
        P(island, None, tensor),
        P(island, None, tensor),
        P(island, None),
        P(None, tensor),
        P(None, tensor),
        P(None, tensor, None),
    )
    out_specs = (P(None, tensor), P(None, tensor))
    return jax.shard_map(local, mesh=fine, in_specs=in_specs, out_specs=out_specs, check_vma=False)
```

```python
import functools
import math

import jax
import jax.numpy as jnp
import numpy as np
from jax import lax
from jax.experimental import pallas as pl
from jax.experimental.pallas import tpu as pltpu
from jax.sharding import Mesh
from jax.sharding import PartitionSpec as P

HEAD_DIM = 128
KEEP = 8
SPAN = 512
ROWS = 128
STORE = 512

inner_rate = 0.01
outer_rate = 0.7
momentum_beta = 0.9
masked_score = -1e30
exp2_scale = HEAD_DIM ** (-0.5) / math.log(2.0)

BF16 = jnp.bfloat16
F32 = jnp.float32
LAST = (((1,), (1,)), ((), ()))
PLAIN = (((1,), (0,)), ((), ()))
FIRST = (((0,), (0,)), ((), ()))
MIB = 1 << 20


def dot(a, b, dims):
    return lax.dot_general(a, b, dims, preferred_element_type=F32)


def dct_tables():
    frequency = np.arange(HEAD_DIM, dtype=np.float64)[:, None]
    sample = np.arange(HEAD_DIM, dtype=np.float64)[None, :]
    basis = np.cos(np.pi * (sample + 0.5) * frequency / HEAD_DIM)
    table = basis * np.where(frequency == 0.0, math.sqrt(1.0 / HEAD_DIM), math.sqrt(2.0 / HEAD_DIM))
    high = table.astype(jnp.bfloat16)
    low = (table - high.astype(np.float64)).astype(jnp.bfloat16)
    return np.concatenate([high, low])


def grads_kernel(
    core_ref, doc_hbm, q_hbm, k_hbm, g_hbm, index_hbm, out_ref, doc_ref, q_ref, k_ref, g_ref, index_ref, cap_ref, total_ref, sems
):
    length = k_ref.shape[0]
    group = q_ref.shape[1] // HEAD_DIM
    half = index_ref.shape[1]
    at = pl.multiple_of(core_ref[0] * half, 128)
    copies = [
        pltpu.make_async_copy(source, target, sems.at[n])
        for n, (source, target) in enumerate(
            (
                (doc_hbm, doc_ref),
                (k_hbm, k_ref),
                (q_hbm, q_ref),
                (g_hbm, g_ref),
                (index_hbm.at[:, pl.ds(at, half)], index_ref),
            )
        )
    ]
    for copy in copies:
        copy.start()
    total_ref[...] = jnp.zeros_like(total_ref)
    copies[0].wait()
    docs = doc_ref[...]
    first = jnp.zeros_like(docs)
    for ident in (1, 2, 3):
        before = jnp.sum((docs < ident).astype(jnp.int32), axis=1, keepdims=True)
        first = jnp.where(docs == ident, before, first)
    blocks = []
    place = 0
    for row in range(0, length, ROWS):
        low = max(0, row - SPAN)
        width = row + ROWS - low
        start = first[:, row : row + ROWS]
        key = lax.broadcasted_iota(jnp.int32, (width, ROWS), 0) + low
        query = lax.broadcasted_iota(jnp.int32, (ROWS, ROWS), 1) + row
        allowed = key >= start
        corner = allowed[width - ROWS :] & (key[width - ROWS :] <= query)
        top = jnp.finfo(F32).max
        if width > ROWS:
            cap_ref[place : place + width - ROWS] = jnp.where(allowed[: width - ROWS], top, masked_score)
        cap_ref[place + width - ROWS : place + width] = jnp.where(corner, top, masked_score)
        blocks.append((row, low, place, place + width))
        place += width
    copies[1].wait()
    copies[2].wait()
    for row, low, begin, end in blocks:
        for head in range(group):
            lanes = slice(head * HEAD_DIM, (head + 1) * HEAD_DIM)
            scores = dot(k_ref[low : row + ROWS], q_ref[row : row + ROWS, lanes], LAST)
            scores = jnp.minimum(scores, cap_ref[begin:end])
            peak = jnp.max(scores, axis=0, keepdims=True)
            weights = jnp.exp2((scores - peak) * exp2_scale)
            inverse = 1.0 / jnp.sum(weights, axis=0, keepdims=True)
            probs = (weights * inverse).astype(BF16)
            if row == 0 and head == 0:
                copies[3].wait()
            total_ref[low : row + ROWS] += dot(probs, g_ref[row : row + ROWS, lanes], PLAIN)
    copies[4].wait()
    section = half // 4
    pieces = []
    for quarter in range(2):
        for c in range(section // 128):
            for side in range(2):
                lane = (2 * quarter + side) * section + c * 128
                pieces.append(index_ref[:, lane : lane + 128])
    index = jnp.concatenate(pieces, axis=0).astype(F32).astype(BF16)
    parts = out_ref.shape[0]
    part = length // parts
    for p in range(parts):
        out_ref[p, :part] = total_ref[p * part : (p + 1) * part].astype(BF16)
        out_ref[p, part:] = index


def in_hbm(*arrays):
    return [pltpu.with_memory_space_constraint(x, pltpu.HBM) for x in arrays]


def in_vmem(*arrays):
    return [pltpu.with_memory_space_constraint(x, pltpu.VMEM) for x in arrays]


HBM = pl.BlockSpec(memory_space=pltpu.HBM)
VMEM = pl.BlockSpec(memory_space=pltpu.VMEM)
SMEM = pl.BlockSpec(memory_space=pltpu.SMEM)


def value_grads(core, doc_ids, queries, key_states, out_grads, index, parts):
    length = key_states.shape[0]
    part = length // parts
    half = index.shape[1] // 2
    index_rows = half * KEEP // 128
    return pl.pallas_call(
        grads_kernel,
        out_shape=jax.ShapeDtypeStruct((parts, part + index_rows, HEAD_DIM), BF16),
        in_specs=[SMEM] + [HBM] * 5,
        out_specs=VMEM,
        scratch_shapes=[
            pltpu.VMEM(doc_ids.shape, jnp.int32),
            pltpu.VMEM(queries.shape, BF16),
            pltpu.VMEM(key_states.shape, BF16),
            pltpu.VMEM(out_grads.shape, BF16),
            pltpu.VMEM((KEEP, half), jnp.int32),
            pltpu.VMEM((sum(min(row, SPAN) + ROWS for row in range(0, length, ROWS)), ROWS), F32),
            pltpu.VMEM((length, HEAD_DIM), F32),
            pltpu.SemaphoreType.DMA((5,)),
        ],
        compiler_params=pltpu.CompilerParams(vmem_limit_bytes=16 * MIB),
    )(core, *in_hbm(doc_ids, queries, key_states, out_grads, index))


def encode_kernel(
    core_ref,
    own_ref,
    other_ref,
    hid_own_ref,
    hid_other_ref,
    table_ref,
    kept_ref,
    table_out_ref,
    wave_ref,
):
    table_out_ref[...] = table_ref[...]
    heads = own_ref.shape[0]
    part = other_ref.shape[1]
    half = hid_own_ref.shape[1] // 2
    section = half // 4
    chunks = section // 128
    for h in range(heads):
        values = jnp.concatenate([own_ref[h, :part], other_ref[h]], axis=0)
        wave = dot(table_ref[:HEAD_DIM], values, LAST) + dot(table_ref[HEAD_DIM:], values, LAST)
        wave_ref[h] = wave.astype(BF16)
    for n in range(2 * chunks):
        quarter, c = divmod(n, chunks)
        at = core_ref[0] * half + quarter * (2 * section) + c * 128
        first, second = (pl.ds(pl.multiple_of(at + side * section, 128), 128) for side in range(2))
        rows = [jnp.concatenate([ref[:, first], ref[:, second]], axis=1) for ref in (hid_own_ref, hid_other_ref)]
        rows = jnp.concatenate(rows, axis=0)
        for h in range(heads):
            coeffs = dot(wave_ref[h], rows, PLAIN)
            index = own_ref[h, part + n * 16 : part + (n + 1) * 16].astype(F32).astype(jnp.int32)
            kept = []
            for side in range(2):
                mine = index[side * 8 : side * 8 + 8]
                block, within = mine >> 3, mine & 7
                found = jnp.zeros((8, 128), F32)
                for v in range(HEAD_DIM // 8):
                    piece = coeffs[v * 8 : v * 8 + 8, side * 128 : side * 128 + 128]
                    found = jnp.where(block == v, jnp.take_along_axis(piece, within, axis=0), found)
                kept.append(found)
            kept_ref[h, quarter, :, c * 128 : (c + 1) * 128] = jnp.concatenate(kept, axis=0).astype(BF16)


def encode(core, own, other, hid_own, hid_other, table):
    heads, part = own.shape[0], other.shape[1]
    return pl.pallas_call(
        encode_kernel,
        out_shape=(
            jax.ShapeDtypeStruct((heads, 2, 2 * KEEP, hid_own.shape[1] // 8), BF16),
            jax.ShapeDtypeStruct(table.shape, BF16),
        ),
        in_specs=[SMEM] + [VMEM] * 5,
        out_specs=(VMEM, VMEM),
        scratch_shapes=[pltpu.VMEM((heads, HEAD_DIM, 2 * part), BF16)],
        compiler_params=pltpu.CompilerParams(vmem_limit_bytes=16 * MIB),
    )(core, *in_vmem(own, other, hid_own, hid_other, table))


def spread(kept, copies):
    total = lax.optimization_barrier(jnp.sum(kept.astype(F32), axis=0)).astype(BF16)
    return jnp.broadcast_to(total[None], (copies,) + total.shape)


def update_rows(scale, base, row, kept_ref, index_ref, table_ref, momentum_ref, weight_ref, new_weight_ref, new_momentum_ref):
    frequency = lax.broadcasted_iota(jnp.int32, (HEAD_DIM, 128), 0).astype(F32).astype(BF16)
    high_table, low_table = table_ref[:HEAD_DIM], table_ref[HEAD_DIM:]
    section = kept_ref.shape[2]
    rows = slice(row, row + 128)
    there = pl.ds(pl.multiple_of(base + row, 128), 128)
    lane = row % section
    place = row // section % 2 * KEEP
    kept = kept_ref[row // (2 * section), place : place + KEEP, lane : lane + 128] * scale
    kept_high = kept.astype(BF16)
    kept_low = (kept - kept_high.astype(F32)).astype(BF16)
    index = index_ref[:, there].astype(F32).astype(BF16)
    high = jnp.zeros((HEAD_DIM, 128), BF16)
    low = jnp.zeros((HEAD_DIM, 128), BF16)
    for t in range(KEEP):
        here = frequency == index[t : t + 1]
        high = jnp.where(here, kept_high[t : t + 1], high)
        low = jnp.where(here, kept_low[t : t + 1], low)
    delta = dot(high, high_table, FIRST) + dot(low, high_table, FIRST) + dot(high, low_table, FIRST)
    fresh = momentum_beta * momentum_ref[there] + delta
    new_momentum_ref[rows] = fresh
    new_weight_ref[rows] = (
        weight_ref[there].astype(F32) - outer_rate * (delta + momentum_beta * fresh)
    ).astype(BF16)


def update_first_kernel(scale, half_ref, *refs):
    total = refs[-1].shape[0]
    for row in range(0, total, 128):
        update_rows(scale, half_ref[0] * total, row, *refs)


def update_second_kernel(scale, half_ref, *refs):
    operands = refs[:5]
    first_weight_ref, first_momentum_ref, weight_hbm, momentum_hbm, new_weight_ref, new_momentum_ref, sems = refs[5:]
    total = new_weight_ref.shape[0]
    half = half_ref[0]
    copies = []

    def store(source, target, base, row, count):
        rows = pl.ds(pl.multiple_of(base + row, STORE), count)
        copies.append(pltpu.make_async_copy(source.at[pl.ds(row, count)], target.at[rows], sems.at[len(copies)]))
        copies[-1].start()

    store(first_momentum_ref, momentum_hbm, (1 - half) * total, 0, total)
    store(first_weight_ref, weight_hbm, (1 - half) * total, 0, total)
    for row in range(0, total, 128):
        update_rows(scale, half * total, row, *operands, new_weight_ref, new_momentum_ref)
        if (row + 128) % STORE == 0:
            store(new_momentum_ref, momentum_hbm, half * total, row + 128 - STORE, STORE)
            store(new_weight_ref, weight_hbm, half * total, row + 128 - STORE, STORE)
    for copy in copies:
        copy.wait()


def update_first(scale, half, kept, index, table, momentum, weight):
    rows = momentum.shape[0] // 2
    return pl.pallas_call(
        functools.partial(update_first_kernel, scale),
        out_shape=(
            jax.ShapeDtypeStruct((rows, HEAD_DIM), BF16),
            jax.ShapeDtypeStruct((rows, HEAD_DIM), F32),
        ),
        in_specs=[SMEM] + [VMEM] * 5,
        out_specs=(VMEM, VMEM),
        compiler_params=pltpu.CompilerParams(vmem_limit_bytes=16 * MIB),
    )(half, *in_vmem(kept, index, table, momentum, weight))


def update_second(scale, half, kept, index, table, momentum, weight, first_weight, first_momentum):
    rows = momentum.shape[0] // 2
    return pl.pallas_call(
        functools.partial(update_second_kernel, scale),
        out_shape=(jax.ShapeDtypeStruct(weight.shape, BF16), jax.ShapeDtypeStruct(momentum.shape, F32)),
        in_specs=[SMEM] + [VMEM] * 7,
        out_specs=(HBM, HBM),
        scratch_shapes=[
            pltpu.VMEM((rows, HEAD_DIM), BF16),
            pltpu.VMEM((rows, HEAD_DIM), F32),
            pltpu.SemaphoreType.DMA((2 + 2 * rows // STORE,)),
        ],
        compiler_params=pltpu.CompilerParams(vmem_limit_bytes=16 * MIB),
    )(half, *in_vmem(kept, index, table, momentum, weight, first_weight, first_momentum))


def swap(x):
    return lax.ppermute(x, "core", [(0, 1), (1, 0)])


def local(hidden_rows, queries, key_states, out_grads, doc_ids, value_weight, momentum, keep_index):
    tensor, near, ring = ("x", "y_lo"), ("x", "y_lo", "z_lo"), ("y_hi", "z_hi", "z_lo")
    islands = lax.axis_size(ring) * 2
    core = lax.axis_index("core").astype(jnp.int32).reshape(1)
    hid_own = hidden_rows[0]
    hid_other = swap(hid_own)
    part = hid_own.shape[0]
    index = keep_index[:, 0, :].T
    packed = value_grads(core, doc_ids, queries[0], key_states[0], out_grads[0], index, lax.axis_size(tensor))
    packed = lax.all_to_all(packed, tensor, 0, 0, tiled=True)
    other = swap(packed[:, :part])
    kept, table = encode(core, packed, other, hid_own, hid_other, dct_tables())
    kept = kept.reshape((-1,) + kept.shape[2:])
    kept = lax.all_to_all(kept, near, 0, 0, tiled=True)
    kept = lax.all_to_all(spread(kept, lax.axis_size(ring)), ring, 0, 0, tiled=True)
    kept = jnp.sum(kept.reshape((-1, lax.axis_size("z_lo")) + kept.shape[1:]).astype(F32), axis=0)
    operands = (index, table, momentum, value_weight)
    first = update_first(inner_rate / islands, core, kept, *operands)
    return update_second(inner_rate / islands, 1 - core, swap(kept), *operands, *first)


def solution(mesh):
    island, tensor = ("z_hi", "z_lo", "y_hi", "core"), ("x", "y_lo")
    fine = Mesh(mesh.devices.reshape(-1, 2, 2, 2, 4, 2), island + tensor)
    in_specs = (
        P(island, tensor, None),
        P(island, None, tensor),
        P(island, None, tensor),
        P(island, None, tensor),
        P(island, None),
        P(None, tensor),
        P(None, tensor),
        P(None, tensor, None),
    )
    out_specs = (P(None, tensor), P(None, tensor))
    return jax.shard_map(local, mesh=fine, in_specs=in_specs, out_specs=out_specs, check_vma=False)
```

```python
import functools
import math

import jax
import jax.numpy as jnp
import numpy as np
from jax import lax
from jax.experimental import pallas as pl
from jax.experimental.pallas import tpu as pltpu
from jax.sharding import Mesh
from jax.sharding import PartitionSpec as P

HEAD_DIM = 128
KEEP = 8
SPAN = 512
ROWS = 128
STORE = 256

inner_rate = 0.01
outer_rate = 0.7
momentum_beta = 0.9
masked_score = -1e30
exp2_scale = HEAD_DIM ** (-0.5) / math.log(2.0)

BF16 = jnp.bfloat16
F32 = jnp.float32
LAST = (((1,), (1,)), ((), ()))
PLAIN = (((1,), (0,)), ((), ()))
FIRST = (((0,), (0,)), ((), ()))
MIB = 1 << 20


def dot(a, b, dims):
    return lax.dot_general(a, b, dims, preferred_element_type=F32)


def dct_tables():
    frequency = np.arange(HEAD_DIM, dtype=np.float64)[:, None]
    sample = np.arange(HEAD_DIM, dtype=np.float64)[None, :]
    basis = np.cos(np.pi * (sample + 0.5) * frequency / HEAD_DIM)
    table = basis * np.where(frequency == 0.0, math.sqrt(1.0 / HEAD_DIM), math.sqrt(2.0 / HEAD_DIM))
    high = table.astype(jnp.bfloat16)
    low = (table - high.astype(np.float64)).astype(jnp.bfloat16)
    return np.concatenate([high, low])


def grads_kernel(
    core_ref, doc_hbm, q_hbm, k_hbm, g_hbm, index_hbm, out_ref, doc_ref, q_ref, k_ref, g_ref, index_ref, cap_ref, total_ref, sems
):
    length = k_ref.shape[0]
    group = q_ref.shape[1] // HEAD_DIM
    half = index_ref.shape[1]
    at = pl.multiple_of(core_ref[0] * half, 128)
    copies = [
        pltpu.make_async_copy(source, target, sems.at[n])
        for n, (source, target) in enumerate(
            (
                (doc_hbm, doc_ref),
                (k_hbm, k_ref),
                (q_hbm, q_ref),
                (g_hbm, g_ref),
                (index_hbm.at[:, pl.ds(at, half)], index_ref),
            )
        )
    ]
    for copy in copies:
        copy.start()
    total_ref[...] = jnp.zeros_like(total_ref)
    copies[0].wait()
    docs = doc_ref[...]
    first = jnp.zeros_like(docs)
    for ident in (1, 2, 3):
        before = jnp.sum((docs < ident).astype(jnp.int32), axis=1, keepdims=True)
        first = jnp.where(docs == ident, before, first)
    blocks = []
    place = 0
    for row in range(0, length, ROWS):
        low = max(0, row - SPAN)
        width = row + ROWS - low
        start = first[:, row : row + ROWS]
        key = lax.broadcasted_iota(jnp.int32, (width, ROWS), 0) + low
        query = lax.broadcasted_iota(jnp.int32, (ROWS, ROWS), 1) + row
        allowed = key >= start
        corner = allowed[width - ROWS :] & (key[width - ROWS :] <= query)
        top = jnp.finfo(F32).max
        if width > ROWS:
            cap_ref[place : place + width - ROWS] = jnp.where(allowed[: width - ROWS], top, masked_score)
        cap_ref[place + width - ROWS : place + width] = jnp.where(corner, top, masked_score)
        blocks.append((row, low, place, place + width))
        place += width
    copies[1].wait()
    copies[2].wait()
    for row, low, begin, end in blocks:
        for head in range(group):
            lanes = slice(head * HEAD_DIM, (head + 1) * HEAD_DIM)
            scores = dot(k_ref[low : row + ROWS], q_ref[row : row + ROWS, lanes], LAST)
            scores = jnp.minimum(scores, cap_ref[begin:end])
            peak = jnp.max(scores, axis=0, keepdims=True)
            weights = jnp.exp2((scores - peak) * exp2_scale)
            inverse = 1.0 / jnp.sum(weights, axis=0, keepdims=True)
            probs = (weights * inverse).astype(BF16)
            if row == 0 and head == 0:
                copies[3].wait()
            total_ref[low : row + ROWS] += dot(probs, g_ref[row : row + ROWS, lanes], PLAIN)
    copies[4].wait()
    section = half // 4
    pieces = []
    for quarter in range(2):
        for c in range(section // 128):
            for side in range(2):
                lane = (2 * quarter + side) * section + c * 128
                pieces.append(index_ref[:, lane : lane + 128])
    index = jnp.concatenate(pieces, axis=0).astype(F32).astype(BF16)
    parts = out_ref.shape[0]
    part = length // parts
    for p in range(parts):
        out_ref[p, :part] = total_ref[p * part : (p + 1) * part].astype(BF16)
        out_ref[p, part:] = index


def in_hbm(*arrays):
    return [pltpu.with_memory_space_constraint(x, pltpu.HBM) for x in arrays]


def in_vmem(*arrays):
    return [pltpu.with_memory_space_constraint(x, pltpu.VMEM) for x in arrays]


HBM = pl.BlockSpec(memory_space=pltpu.HBM)
VMEM = pl.BlockSpec(memory_space=pltpu.VMEM)
SMEM = pl.BlockSpec(memory_space=pltpu.SMEM)


def value_grads(core, doc_ids, queries, key_states, out_grads, index, parts):
    length = key_states.shape[0]
    part = length // parts
    half = index.shape[1] // 2
    index_rows = half * KEEP // 128
    return pl.pallas_call(
        grads_kernel,
        out_shape=jax.ShapeDtypeStruct((parts, part + index_rows, HEAD_DIM), BF16),
        in_specs=[SMEM] + [HBM] * 5,
        out_specs=VMEM,
        scratch_shapes=[
            pltpu.VMEM(doc_ids.shape, jnp.int32),
            pltpu.VMEM(queries.shape, BF16),
            pltpu.VMEM(key_states.shape, BF16),
            pltpu.VMEM(out_grads.shape, BF16),
            pltpu.VMEM((KEEP, half), jnp.int32),
            pltpu.VMEM((sum(min(row, SPAN) + ROWS for row in range(0, length, ROWS)), ROWS), F32),
            pltpu.VMEM((length, HEAD_DIM), F32),
            pltpu.SemaphoreType.DMA((5,)),
        ],
        compiler_params=pltpu.CompilerParams(vmem_limit_bytes=16 * MIB),
    )(core, *in_hbm(doc_ids, queries, key_states, out_grads, index))


def encode_kernel(
    core_ref,
    own_ref,
    other_ref,
    hid_own_ref,
    hid_other_ref,
    table_ref,
    kept_ref,
    table_out_ref,
    wave_ref,
):
    table_out_ref[...] = table_ref[...]
    heads = own_ref.shape[0]
    part = other_ref.shape[1]
    half = hid_own_ref.shape[1] // 2
    section = half // 4
    chunks = section // 128
    for h in range(heads):
        values = jnp.concatenate([own_ref[h, :part], other_ref[h]], axis=0)
        wave = dot(table_ref[:HEAD_DIM], values, LAST) + dot(table_ref[HEAD_DIM:], values, LAST)
        wave_ref[h] = wave.astype(BF16)
    for n in range(2 * chunks):
        quarter, c = divmod(n, chunks)
        at = core_ref[0] * half + quarter * (2 * section) + c * 128
        first, second = (pl.ds(pl.multiple_of(at + side * section, 128), 128) for side in range(2))
        rows = [jnp.concatenate([ref[:, first], ref[:, second]], axis=1) for ref in (hid_own_ref, hid_other_ref)]
        rows = jnp.concatenate(rows, axis=0)
        for h in range(heads):
            coeffs = dot(wave_ref[h], rows, PLAIN)
            index = own_ref[h, part + n * 16 : part + (n + 1) * 16].astype(F32).astype(jnp.int32)
            kept = []
            for side in range(2):
                mine = index[side * 8 : side * 8 + 8]
                block, within = mine >> 3, mine & 7
                found = jnp.zeros((8, 128), F32)
                for v in range(HEAD_DIM // 8):
                    piece = coeffs[v * 8 : v * 8 + 8, side * 128 : side * 128 + 128]
                    found = jnp.where(block == v, jnp.take_along_axis(piece, within, axis=0), found)
                kept.append(found)
            kept_ref[h, quarter, :, c * 128 : (c + 1) * 128] = jnp.concatenate(kept, axis=0).astype(BF16)


def encode(core, own, other, hid_own, hid_other, table):
    heads, part = own.shape[0], other.shape[1]
    return pl.pallas_call(
        encode_kernel,
        out_shape=(
            jax.ShapeDtypeStruct((heads, 2, 2 * KEEP, hid_own.shape[1] // 8), BF16),
            jax.ShapeDtypeStruct(table.shape, BF16),
        ),
        in_specs=[SMEM] + [VMEM] * 5,
        out_specs=(VMEM, VMEM),
        scratch_shapes=[pltpu.VMEM((heads, HEAD_DIM, 2 * part), BF16)],
        compiler_params=pltpu.CompilerParams(vmem_limit_bytes=16 * MIB),
    )(core, *in_vmem(own, other, hid_own, hid_other, table))


def spread(kept, copies):
    total = lax.optimization_barrier(jnp.sum(kept.astype(F32), axis=0)).astype(BF16)
    return jnp.broadcast_to(total[None], (copies,) + total.shape)


def update_rows(scale, base, row, kept_ref, index_ref, table_ref, momentum_ref, weight_ref, new_weight_ref, new_momentum_ref):
    frequency = lax.broadcasted_iota(jnp.int32, (HEAD_DIM, 128), 0).astype(F32).astype(BF16)
    high_table, low_table = table_ref[:HEAD_DIM], table_ref[HEAD_DIM:]
    section = kept_ref.shape[2]
    rows = slice(row, row + 128)
    there = pl.ds(pl.multiple_of(base + row, 128), 128)
    lane = row % section
    place = row // section % 2 * KEEP
    kept = kept_ref[row // (2 * section), place : place + KEEP, lane : lane + 128] * scale
    kept_high = kept.astype(BF16)
    kept_low = (kept - kept_high.astype(F32)).astype(BF16)
    index = index_ref[:, there].astype(F32).astype(BF16)
    high = jnp.zeros((HEAD_DIM, 128), BF16)
    low = jnp.zeros((HEAD_DIM, 128), BF16)
    for t in range(KEEP):
        here = frequency == index[t : t + 1]
        high = jnp.where(here, kept_high[t : t + 1], high)
        low = jnp.where(here, kept_low[t : t + 1], low)
    delta = dot(high, high_table, FIRST) + dot(low, high_table, FIRST) + dot(high, low_table, FIRST)
    fresh = momentum_beta * momentum_ref[there] + delta
    new_momentum_ref[rows] = fresh
    new_weight_ref[rows] = (
        weight_ref[there].astype(F32) - outer_rate * (delta + momentum_beta * fresh)
    ).astype(BF16)


def update_first_kernel(scale, half_ref, *refs):
    total = refs[-1].shape[0]
    for row in range(0, total, 128):
        update_rows(scale, half_ref[0] * total, row, *refs)


def update_second_kernel(scale, half_ref, *refs):
    operands = refs[:5]
    first_weight_ref, first_momentum_ref, weight_hbm, momentum_hbm, new_weight_ref, new_momentum_ref, sems = refs[5:]
    total = new_weight_ref.shape[0]
    half = half_ref[0]
    copies = []

    def store(source, target, base, row, count):
        rows = pl.ds(pl.multiple_of(base + row, STORE), count)
        copies.append(pltpu.make_async_copy(source.at[pl.ds(row, count)], target.at[rows], sems.at[len(copies)]))
        copies[-1].start()

    store(first_momentum_ref, momentum_hbm, (1 - half) * total, 0, total)
    store(first_weight_ref, weight_hbm, (1 - half) * total, 0, total)
    for row in range(0, total, 128):
        update_rows(scale, half * total, row, *operands, new_weight_ref, new_momentum_ref)
        if (row + 128) % STORE == 0:
            store(new_momentum_ref, momentum_hbm, half * total, row + 128 - STORE, STORE)
            store(new_weight_ref, weight_hbm, half * total, row + 128 - STORE, STORE)
    for copy in copies:
        copy.wait()


def update_first(scale, half, kept, index, table, momentum, weight):
    rows = momentum.shape[0] // 2
    return pl.pallas_call(
        functools.partial(update_first_kernel, scale),
        out_shape=(
            jax.ShapeDtypeStruct((rows, HEAD_DIM), BF16),
            jax.ShapeDtypeStruct((rows, HEAD_DIM), F32),
        ),
        in_specs=[SMEM] + [VMEM] * 5,
        out_specs=(VMEM, VMEM),
        compiler_params=pltpu.CompilerParams(vmem_limit_bytes=16 * MIB),
    )(half, *in_vmem(kept, index, table, momentum, weight))


def update_second(scale, half, kept, index, table, momentum, weight, first_weight, first_momentum):
    rows = momentum.shape[0] // 2
    return pl.pallas_call(
        functools.partial(update_second_kernel, scale),
        out_shape=(jax.ShapeDtypeStruct(weight.shape, BF16), jax.ShapeDtypeStruct(momentum.shape, F32)),
        in_specs=[SMEM] + [VMEM] * 7,
        out_specs=(HBM, HBM),
        scratch_shapes=[
            pltpu.VMEM((rows, HEAD_DIM), BF16),
            pltpu.VMEM((rows, HEAD_DIM), F32),
            pltpu.SemaphoreType.DMA((2 + 2 * rows // STORE,)),
        ],
        compiler_params=pltpu.CompilerParams(vmem_limit_bytes=16 * MIB),
    )(half, *in_vmem(kept, index, table, momentum, weight, first_weight, first_momentum))


def swap(x):
    return lax.ppermute(x, "core", [(0, 1), (1, 0)])


def local(hidden_rows, queries, key_states, out_grads, doc_ids, value_weight, momentum, keep_index):
    tensor, near, ring = ("x", "y_lo"), ("x", "y_lo", "z_lo"), ("y_hi", "z_hi", "z_lo")
    islands = lax.axis_size(ring) * 2
    core = lax.axis_index("core").astype(jnp.int32).reshape(1)
    hid_own = hidden_rows[0]
    hid_other = swap(hid_own)
    part = hid_own.shape[0]
    index = keep_index[:, 0, :].T
    packed = value_grads(core, doc_ids, queries[0], key_states[0], out_grads[0], index, lax.axis_size(tensor))
    packed = lax.all_to_all(packed, tensor, 0, 0, tiled=True)
    other = swap(packed[:, :part])
    kept, table = encode(core, packed, other, hid_own, hid_other, dct_tables())
    kept = kept.reshape((-1,) + kept.shape[2:])
    kept = lax.all_to_all(kept, near, 0, 0, tiled=True)
    kept = lax.all_to_all(spread(kept, lax.axis_size(ring)), ring, 0, 0, tiled=True)
    kept = jnp.sum(kept.reshape((-1, lax.axis_size("z_lo")) + kept.shape[1:]).astype(F32), axis=0)
    operands = (index, table, momentum, value_weight)
    first = update_first(inner_rate / islands, core, kept, *operands)
    return update_second(inner_rate / islands, 1 - core, swap(kept), *operands, *first)


def solution(mesh):
    island, tensor = ("z_hi", "z_lo", "y_hi", "core"), ("x", "y_lo")
    fine = Mesh(mesh.devices.reshape(-1, 2, 2, 2, 4, 2), island + tensor)
    in_specs = (
        P(island, tensor, None),
        P(island, None, tensor),
        P(island, None, tensor),
        P(island, None, tensor),
        P(island, None),
        P(None, tensor),
        P(None, tensor),
        P(None, tensor, None),
    )
    out_specs = (P(None, tensor), P(None, tensor))
    return jax.shard_map(local, mesh=fine, in_specs=in_specs, out_specs=out_specs, check_vma=False)
```
